256 devices in a mesh: gx: 16 (over z_hi, x), gy: 16 (over y, z_lo, core).
Axes of the slice: x: 4, y: 4, z: 8 (z_hi: 4, z_lo: 2; z = z_hi * 2 + z_lo), core: 2. Of those that a mesh axis runs over, the one named last changes fastest.
Arguments:
- basis_start: float32 [128, 2048, 256], P('gx', 'gy')
- admit: float32 [128, 2048], P('gx', 'gy'), may hold values from 0.5 to 2
- pattern: int32 [128, 2048], P('gx', 'gy'), may hold values 0 or 1
- ground: float32 [128, 2048], P('gx', 'gy'), may hold values from 0.2 to 2
- capacity: float32 [128, 2048], P('gx', 'gy'), may hold values from 0.5 to 2
- ports: int32 [2048], P(('gx', 'gy')), may hold values from 0 to 1023
- drive: float32 [2048, 64], P(('gx', 'gy')), may hold values from -6 to 6
- corner_table: int32 [32, 3], P('gy'), may hold values from 0 to 3
- level_table: float32 [3, 4], replicated, may hold values from 0.5 to 2
Outputs:
- basis_next: float32 [128, 2048, 256], P('gx', 'gy')
- response: float32 [32, 64, 512], P('gy')
The draws below stay inside these ranges and needn't reach their ends.
Inputs may be any that keep to these rules, and one draw needn't show every extreme that they name: `ports`: driver d's node index counts row-major inside the tile of 8 x 128 nodes held by device d // 8.
All inputs are finite; a program needn't handle non-finite values. No bound on the sum of `pattern` on one device may be relied on, other than what follows from the above.
Results may differ from the reference program's by a relative error of at most 0.0003.
Values sent between devices are 32-bit elements; how exact they have to be, the bound alone decides.
A program may use at most 64 MiB of HBM per device.

```python
import math
import jax
import jax.numpy as jnp
from jax import lax

K = 256
TX = 8
TY = 128
DRV_DEV = 8
STEPS = 64
CORNERS = 32
LEVELS = 4
NX = 128
NY = 2048
DRIVERS = 2048
N_GY = 16


def draw_basis_start(key, part):
    key = jax.random.fold_in(key, 11)
    keys = jax.random.split(key, 3)
    base = jax.random.normal(keys[0], (NX, NY, K), jnp.float32)
    col_scale = jnp.exp(jax.random.uniform(keys[1], (K,), jnp.float32, 0.0, math.log(10.0)))
    row_scale = jnp.exp(jax.random.uniform(keys[2], (NX, NY, 1), jnp.float32, 0.0, math.log(10.0)))
    return base * row_scale * col_scale


def touch_ends(drawn, stream_key, least, top_value):
    longest = drawn.shape.index(max(drawn.shape))
    spots = []
    for shift in (0, 1):
        where = [jax.random.randint(jax.random.fold_in(stream_key, axis), (), 0, length) for axis, length in enumerate(drawn.shape)]
        where[longest] = (where[longest] + shift) % drawn.shape[longest]
        spots.append(tuple(where))
    return drawn.at[spots[0]].set(least).at[spots[1]].set(top_value)


def block_scale(rng, shape, cuts, smallest, high):
    factor_of, own = 1.0, jax.random.fold_in(rng, 6)
    for dim, parts in cuts:
        draws = jnp.exp(jax.random.uniform(jax.random.fold_in(own, dim), (parts,), jnp.float32, smallest / len(cuts), high / len(cuts)))
        factor_of = factor_of * jnp.repeat(draws, shape[dim] // parts).reshape([-1 if axis == dim else 1 for axis in range(len(shape))])
    return factor_of


def scatter_about(stream_key, extent, spread, reach, pieces=(), kind=jnp.bfloat16):
    entries = jax.random.normal(stream_key, extent, jnp.float32) * spread
    if len(pieces) > 0:
        entries = block_scale(stream_key, extent, pieces, -0.22, 0.18) * entries
    return jnp.clip(entries, min=-reach, max=reach).astype(kind)


def setup_inputs(seed: int = 0) -> dict:
    seeds = jax.random.split(jax.random.key(seed), 10)
    return {
        "basis_start": draw_basis_start(jax.random.fold_in(seeds[9], 71), 0),
        "admit": jnp.clip(jnp.exp(math.log(2.0) - 1.3862944 * jax.random.uniform(seeds[1], (NX, NY), jnp.float32) ** block_scale(seeds[1], (NX, NY), ((0, 16), (1, 16)), -0.2, 0.2)), 0.5, 2.0),
        "pattern": touch_ends((jax.random.randint(seeds[2], (NX, NY), 0, 8) < 7).astype(jnp.int32), jax.random.fold_in(seeds[2], 1), 0, 1),
        "ground": jnp.clip(jnp.exp(math.log(2.0) - 2.3025851 * jax.random.uniform(seeds[3], (NX, NY), jnp.float32) ** block_scale(seeds[3], (NX, NY), ((0, 16), (1, 16)), -0.2, 0.2)), 0.2, 2.0),
        "capacity": jnp.clip(jnp.exp(math.log(2.0) - 1.3862944 * jax.random.uniform(seeds[4], (NX, NY), jnp.float32) ** block_scale(seeds[4], (NX, NY), ((0, 16), (1, 16)), -0.2, 0.2)), 0.5, 2.0),
        "ports": touch_ends(jax.random.randint(seeds[5], (DRIVERS,), 0, TX * TY), jax.random.fold_in(seeds[5], 1), 0, (TX * TY) - 1).astype(jnp.int32),
        "drive": scatter_about(seeds[6], (DRIVERS, STEPS), 1.0, 6.0, ((0, 256),), jnp.float32),
        "corner_table": touch_ends(jax.random.randint(seeds[7], (CORNERS, 3), 0, LEVELS), jax.random.fold_in(seeds[7], 1), 0, LEVELS - 1).astype(jnp.int32),
        "level_table": jnp.clip(jnp.exp(jax.random.uniform(seeds[8], (3, LEVELS), jnp.float32, math.log(0.5), math.log(2.0))), 0.5, 2.0),
    }


highest = lax.Precision.HIGHEST
time_step = 0.25

def neighbour_sum(padded):
    return padded[2:, 1:-1] + padded[:-2, 1:-1] + padded[1:-1, 2:] + padded[1:-1, :-2]

def product(left_op, right_op):
    return jnp.dot(left_op, right_op, precision=highest)

def mesh_product(column_block, strength, diagonal):
    pad_width = ((1, 1), (1, 1), (0, 0))
    neighbours = neighbour_sum(jnp.pad(strength[:, :, None] * column_block, pad_width))
    return diagonal[:, :, None] * column_block - strength[:, :, None] * neighbours

def orthonormal(flat_rows, gram_sum, node_count):
    factor_low = jnp.linalg.cholesky(gram_sum / node_count)
    return jax.scipy.linalg.solve_triangular(factor_low, flat_rows.T, lower=True).T

def corner_scales(corner_table, level_table):
    level_ids = jnp.arange(level_table.shape[1], dtype=jnp.int32)
    onehot = (corner_table[:, :, None] == level_ids[None, None, :]).astype(jnp.float32)
    return lax.optimization_barrier(jnp.sum(onehot * level_table[None, :, :], axis=2))

def transient(gred, cred, forcing, scales):

    def one_corner(corner):
        cap_ratio = corner[1] / time_step
        system = corner[0] * gred + cap_ratio * cred
        factor = jnp.linalg.cholesky(system)
        carry_map = jax.scipy.linalg.cho_solve((factor, True), cap_ratio * cred)
        forced = jax.scipy.linalg.cho_solve((factor, True), corner[2] * forcing)
        return (carry_map, forced.T)
    carry_maps, forced = jax.vmap(one_corner)(scales)

    def advance(voltage, drive_now):
        voltage = jnp.einsum('kij,kj->ki', carry_maps, voltage, precision=highest) + drive_now
        return (voltage, voltage)
    initial = jnp.zeros((scales.shape[0], gred.shape[0]), jnp.float32)
    final_state, states = lax.scan(advance, initial, jnp.transpose(forced, (1, 0, 2)))
    return jnp.transpose(states, (1, 0, 2))

def reference(basis_start, admit, pattern, ground, capacity, ports, drive, corner_table, level_table):
    node_count = NX * NY
    strength = admit * pattern.astype(jnp.float32)
    diagonal = ground + strength * neighbour_sum(jnp.pad(strength, 1))
    flat_start = basis_start.reshape(node_count, K)
    first = orthonormal(flat_start, product(flat_start.T, flat_start), node_count)
    image_first = mesh_product(first.reshape(NX, NY, K), strength, diagonal).reshape(node_count, K)
    flat_cap = capacity.reshape(node_count, 1)
    krylov = image_first / flat_cap
    coeffs = product(first.T, krylov) / node_count
    residue = krylov - product(first, coeffs)
    second = orthonormal(residue, product(residue.T, residue), node_count)
    image_second = mesh_product(second.reshape(NX, NY, K), strength, diagonal).reshape(node_count, K)
    cond_head = product(first.T, image_first)
    cond_cross = product(first.T, image_second)
    cond_back = product(second.T, image_first)
    cond_tail = product(second.T, image_second)
    cap_first = flat_cap * first
    cap_second = flat_cap * second
    cap_head = product(first.T, cap_first)
    cap_cross = product(first.T, cap_second)
    cap_back = product(second.T, cap_first)
    cap_tail = product(second.T, cap_second)
    gred = jnp.concatenate([jnp.concatenate([cond_head, cond_cross], 1), jnp.concatenate([cond_back, cond_tail], 1)], 0) / node_count
    cred = jnp.concatenate([jnp.concatenate([cap_head, cap_cross], 1), jnp.concatenate([cap_back, cap_tail], 1)], 0) / node_count
    device = jnp.arange(DRIVERS, dtype=jnp.int32) // DRV_DEV
    node_row = device // N_GY * TX + ports // TY
    node_col = device % N_GY * TY + ports % TY
    flat_index = (node_row * NY + node_col).astype(jnp.int32)
    port_rows = jnp.concatenate([jnp.take(first, flat_index, axis=0), jnp.take(second, flat_index, axis=0)], 1)
    forcing = product(port_rows.T, drive) / math.sqrt(DRIVERS)
    scales = corner_scales(corner_table, level_table)
    response = transient(gred, cred, forcing, scales)
    return (second.reshape(NX, NY, K), response)
```

```python
import functools
import math

import jax
import jax.numpy as jnp
from jax import lax
from jax.experimental import pallas as pl
from jax.experimental.pallas import tpu as pltpu
from jax.sharding import PartitionSpec as P

MESH = pl.DeviceIdType.MESH
highest = lax.Precision.HIGHEST
time_step = 0.25
K = 256
TX = 8
TY = 128
NODES = TX * TY
STEPS = 64
BLOCK = 128
ROWS = 4096


def dot(a, b, ca=1, cb=0, precision=highest):
    return lax.dot_general(
        a, b, (((ca,), (cb,)), ((), ())), precision=precision, preferred_element_type=jnp.float32
    )


def place():
    gx, gy = lax.axis_index("gx"), lax.axis_index("gy")
    z = (gx // 4) * 2 + (gy % 4) // 2
    return gx, gy, gx % 4, gy // 4, z, gy % 2


def device(x, y, z, core):
    return ((z // 2) * 4 + x, y * 4 + (z % 2) * 2 + core)


def stats_kernel(
    basis, admit, pattern, ground, capacity, ports, drive,
    y_out, out,
    strength, sx, left_send, right_send, tiles, halo_row, halo_col,
    top_send, edge_send, next_row, next_col,
    v, got0, got1, got2, got3, send_sem, recv_sem,
):
    gx, gy, x, y, z, core = place()
    up = (lax.rem(gx + 15, 16), gy)
    down = (lax.rem(gx + 1, 16), gy)
    left = (gx, lax.rem(gy + 15, 16))
    right = (gx, lax.rem(gy + 1, 16))
    sibling = device(x, y, z, 1 - core)
    along_x = [device(lax.rem(x + d, 4), y, z, core) for d in range(1, 4)]
    along_y = [device(x, lax.rem(y + d, 4), z, core) for d in range(1, 4)]
    along_z = [device(x, y, lax.rem(z + d, 8), core) for d in range(1, 8)]
    barrier = pltpu.get_barrier_semaphore()
    partners = [up, down, left, right, sibling] + along_x + along_y + along_z
    for partner in partners:
        pl.semaphore_signal(barrier, inc=1, device_id=partner, device_id_type=MESH)

    started = []

    def send(src, dst, target):
        i = len(started)
        copy = pltpu.make_async_remote_copy(
            src_ref=src, dst_ref=dst, send_sem=send_sem.at[i], recv_sem=recv_sem.at[i],
            device_id=target, device_id_type=MESH,
        )
        copy.start()
        started.append(copy)
        return copy

    strength[...] = admit[...] * pattern[...].astype(jnp.float32)
    own = strength[...]
    own_t = own.T
    for r in range(TX):
        rows = pl.ds(r * TY, TY)
        weighted = own_t[:, r : r + 1] * basis[rows, :]
        sx[rows, :] = weighted
        left_send[r : r + 1, :] = weighted[0:1, :]
        right_send[r : r + 1, :] = weighted[TY - 1 : TY, :]
    pl.semaphore_wait(barrier, len(partners))
    last = (TX - 1) * TY
    halo = [
        send(strength, tiles.at[0], down),
        send(strength, tiles.at[1], up),
        send(strength, tiles.at[2], right),
        send(strength, tiles.at[3], left),
        send(sx.at[pl.ds(last, TY), :], halo_row.at[0], down),
        send(sx.at[pl.ds(0, TY), :], halo_row.at[1], up),
        send(right_send, halo_col.at[0], right),
        send(left_send, halo_col.at[1], left),
    ]

    def put(m, value):
        v[pl.ds(m * 512, 256), :] = value[:, :128]
        v[pl.ds(m * 512 + 256, 256), :] = value[:, 128:]

    xt = basis[...].T
    cap = capacity[...]
    cap_t = cap.T
    for r in range(TX):
        rows = pl.ds(r * TY, TY)
        y_out[rows, :] = cap_t[:, r : r + 1] * basis[rows, :]
    put(0, dot(xt, basis[...]))
    put(3, dot(xt, y_out[...]))

    for copy in halo:
        copy.wait_recv()
    has_up, has_down = gx > 0, gx < 15
    has_left, has_right = gy > 0, gy < 15
    above = jnp.where(has_up, tiles[0, TX - 1 : TX, :], 0.0)
    below = jnp.where(has_down, tiles[1, 0:1, :], 0.0)
    before = jnp.where(has_left, tiles[2, :, TY - 1 : TY], 0.0)
    after = jnp.where(has_right, tiles[3, :, 0:1], 0.0)
    degree = (
        jnp.concatenate([above, own[:-1]], 0)
        + jnp.concatenate([own[1:], below], 0)
        + jnp.concatenate([before, own[:, :-1]], 1)
        + jnp.concatenate([own[:, 1:], after], 1)
    )
    diagonal = ground[...] + own * degree
    diagonal_t = diagonal.T
    place_in_row = lax.broadcasted_iota(jnp.int32, (TY, K), 0)

    def moved_back(block, edge):
        return jnp.where(place_in_row == TY - 1, edge, pltpu.roll(block, TY - 1, 0))

    def moved_on(block, edge):
        return jnp.where(place_in_row == 0, edge, pltpu.roll(block, 1, 0))

    halo_up = jnp.where(has_up, halo_row[0], 0.0)
    halo_down = jnp.where(has_down, halo_row[1], 0.0)
    halo_left = jnp.where(has_left, halo_col[0], 0.0)
    halo_right = jnp.where(has_right, halo_col[1], 0.0)
    for r in range(TX):
        rows = pl.ds(r * TY, TY)
        here = sx[rows, :]
        total = moved_on(here, halo_left[r : r + 1]) + moved_back(here, halo_right[r : r + 1])
        total = total + (halo_up if r == 0 else sx[pl.ds((r - 1) * TY, TY), :])
        total = total + (halo_down if r == TX - 1 else sx[pl.ds((r + 1) * TY, TY), :])
        image = diagonal_t[:, r : r + 1] * basis[rows, :] - own_t[:, r : r + 1] * total
        krylov = image / cap_t[:, r : r + 1]
        y_out[rows, :] = krylov
        weighted = own_t[:, r : r + 1] * krylov
        if r == 0:
            top_send[...] = weighted
        edge_send[r : r + 1, :] = weighted[0:1, :]
    border = [send(top_send, next_row, up), send(edge_send, next_col, left)]

    put(1, dot(xt, y_out[...]))
    yt = y_out[...].T
    put(2, dot(yt, y_out[...]))
    cap_y = jnp.concatenate(
        [cap_t[:, r : r + 1] * y_out[pl.ds(r * TY, TY), :] for r in range(TX)], 0
    )
    put(4, dot(xt, cap_y))
    put(5, dot(yt, cap_y))
    node = lax.broadcasted_iota(jnp.int32, (8, NODES), 1)
    driver = lax.broadcasted_iota(jnp.int32, (8, NODES), 0)
    spot = jnp.full((8, NODES), -1, jnp.int32)
    for d in range(8):
        spot = jnp.where(driver == d, ports[d], spot)
    picked = (node == spot).astype(jnp.float32)
    v[pl.ds(3584, 256), 0:STEPS] = dot(dot(picked, basis[...]), drive[...], 0, 0)
    v[pl.ds(3584, 256), STEPS:128] = dot(dot(picked, y_out[...]), drive[...], 0, 0)
    v[pl.ds(3840, 256), :] = jnp.zeros((256, 128), jnp.float32)

    for copy in border:
        copy.wait_recv()
    bottom = jnp.where(has_down, next_row[...], 0.0)
    side = jnp.where(has_right, next_col[...], 0.0)
    for copy in halo:
        copy.wait_send()
    for r in range(TX):
        rows = pl.ds(r * TY, TY)
        here = own_t[:, r : r + 1] * y_out[rows, :]
        sx[rows, :] = here
    for r in range(TX):
        rows = pl.ds(r * TY, TY)
        total = moved_back(sx[rows, :], side[r : r + 1])
        total = total + (bottom if r == TX - 1 else sx[pl.ds((r + 1) * TY, TY), :])
        sx[rows, :] = (
            0.5 * diagonal_t[:, r : r + 1] * y_out[rows, :] - own_t[:, r : r + 1] * total
        )
    put(6, dot(yt, sx[...]))

    mine = core * 2048
    other = (1 - core) * 2048
    a0, b0 = mine, mine + 1024
    a1, b1 = a0 + x * 256, b0 + y * 256
    a2, b2 = a1 + y * 64, b1 + x * 64
    a3, b3 = a2 + z * 8, b2 + z * 8

    def span(ref, start, size):
        return ref.at[pl.ds(pl.multiple_of(start, 8), size), :]

    first = [
        send(span(v, other + h * 1024, 1024), got0.at[h], sibling) for h in range(2)
    ]

    def spread(base, size, line, position, got, ring):
        return [
            send(span(v, base + lax.rem(position + d, ring) * size, size), got.at[d - 1], line[d - 1])
            for d in range(1, ring)
        ]

    def collect(copies, base, size, got, count):
        for copy in copies:
            copy.wait_recv()
        rows = pl.ds(pl.multiple_of(base, 8), size)
        total = v[rows, :]
        for i in range(count):
            total = total + got[i]
        return total

    for h, base in enumerate((a0, b0)):
        first[h].wait_recv()
        rows = pl.ds(pl.multiple_of(base, 8), 1024)
        v[rows, :] = v[rows, :] + got0[h]
        if h == 0:
            one_a = spread(a0, 256, along_x, x, got1.at[0], 4)
        else:
            one_b = spread(b0, 256, along_y, y, got1.at[1], 4)
    v[pl.ds(pl.multiple_of(a1, 8), 256), :] = collect(one_a, a1, 256, got1.at[0], 3)
    two_a = spread(a1, 64, along_y, y, got2.at[0], 4)
    v[pl.ds(pl.multiple_of(b1, 8), 256), :] = collect(one_b, b1, 256, got1.at[1], 3)
    two_b = spread(b1, 64, along_x, x, got2.at[1], 4)
    v[pl.ds(pl.multiple_of(a2, 8), 64), :] = collect(two_a, a2, 64, got2.at[0], 3)
    three_a = spread(a2, 8, along_z, z, got3.at[0], 8)
    v[pl.ds(pl.multiple_of(b2, 8), 64), :] = collect(two_b, b2, 64, got2.at[1], 3)
    three_b = spread(b2, 8, along_z, z, got3.at[1], 8)

    def share(base, size, line):
        return [send(span(out, base, size), span(out, base, size), target) for target in line]

    out[pl.ds(pl.multiple_of(a3, 8), 8), :] = collect(three_a, a3, 8, got3.at[0], 7)
    back_a = share(a3, 8, along_z)
    out[pl.ds(pl.multiple_of(b3, 8), 8), :] = collect(three_b, b3, 8, got3.at[1], 7)
    back_b = share(b3, 8, along_z)
    for copy in back_a:
        copy.wait_recv()
    back_a = share(a2, 64, along_y)
    for copy in back_b:
        copy.wait_recv()
    back_b = share(b2, 64, along_x)
    for copy in back_a:
        copy.wait_recv()
    back_a = share(a1, 256, along_x)
    for copy in back_b:
        copy.wait_recv()
    back_b = share(b1, 256, along_y)
    for copy in back_a:
        copy.wait_recv()
    back_a = share(a0, 1024, [sibling])
    for copy in back_b:
        copy.wait_recv()
    back_b = share(b0, 1024, [sibling])
    for copy in back_a + back_b:
        copy.wait_recv()
    for copy in started[len(halo) :]:
        copy.wait_send()


def stats(basis, admit, pattern, ground, capacity, ports, drive):
    vmem = pl.BlockSpec(memory_space=pltpu.VMEM)
    smem = pl.BlockSpec(memory_space=pltpu.SMEM)
    f32 = jnp.float32
    copies = 8 + 2 + 2 * (2 + 6 + 6 + 14)
    return pl.pallas_call(
        stats_kernel,
        out_shape=(
            jax.ShapeDtypeStruct((NODES, K), f32),
            jax.ShapeDtypeStruct((ROWS, 128), f32),
        ),
        in_specs=[vmem] * 5 + [smem, vmem],
        out_specs=(vmem, vmem),
        scratch_shapes=[
            pltpu.VMEM((TX, TY), f32),
            pltpu.VMEM((NODES, K), f32),
            pltpu.VMEM((TX, K), f32),
            pltpu.VMEM((TX, K), f32),
            pltpu.VMEM((4, TX, TY), f32),
            pltpu.VMEM((2, TY, K), f32),
            pltpu.VMEM((2, TX, K), f32),
            pltpu.VMEM((TY, K), f32),
            pltpu.VMEM((TX, K), f32),
            pltpu.VMEM((TY, K), f32),
            pltpu.VMEM((TX, K), f32),
            pltpu.VMEM((ROWS, 128), f32),
            pltpu.VMEM((2, 1024, 128), f32),
            pltpu.VMEM((2, 3, 256, 128), f32),
            pltpu.VMEM((2, 3, 64, 128), f32),
            pltpu.VMEM((2, 7, 8, 128), f32),
            pltpu.SemaphoreType.DMA((copies,)),
            pltpu.SemaphoreType.DMA((copies,)),
        ],
        compiler_params=pltpu.CompilerParams(
            collective_id=0, has_side_effects=True, vmem_limit_bytes=48 * 1024 * 1024
        ),
        name="stats",
    )(basis, admit, pattern, ground, capacity, ports, drive)


def solve_kernel(
    nodes, drivers, sums, basis, krylov, corners, levels, second, response,
    mats, inv, cap_mat, forcing, work,
):
    scale = 1.0 / nodes

    def take(m):
        return (
            jnp.concatenate([sums[pl.ds(m * 512, 256), :], sums[pl.ds(m * 512 + 256, 256), :]], 1)
            * scale
        )

    xx, xy, yy, xcx, xcy, ycy, half = [take(m) for m in range(7)]
    mats[0, :256, :256] = xx
    mats[0, :256, 256:] = xy
    mats[0, 256:, :256] = xy.T
    mats[0, 256:, 256:] = yy
    cap_mat[:256, :256] = xcx
    cap_mat[:256, 256:] = xcy
    cap_mat[256:, :256] = xcy.T
    cap_mat[256:, 256:] = ycy
    ratios, gains = [], []
    for k in range(2):
        g = levels[0, corners[k, 0]]
        ratio = levels[1, corners[k, 1]] * (1.0 / time_step)
        ratios.append(ratio)
        gains.append(levels[2, corners[k, 2]])
        mats[k + 1, :256, :256] = g * xcy + ratio * xcx
        mats[k + 1, :256, 256:] = g * ycy + ratio * xcy
        mats[k + 1, 256:, :256] = g * ycy.T + ratio * xcy.T
        mats[k + 1, 256:, 256:] = g * (half + half.T) + ratio * ycy
    part = sums[pl.ds(3584, 256), :] * (1.0 / math.sqrt(drivers))
    forcing[:256, :] = part[:, :STEPS]
    forcing[256:, :] = part[:, STEPS:]
    inv[...] = jnp.zeros_like(inv)

    lane = lax.broadcasted_iota(jnp.int32, (8, 128), 1)
    sub = lax.broadcasted_iota(jnp.int32, (8, 256), 0)
    row_id = lax.broadcasted_iota(jnp.int32, (BLOCK, BLOCK), 0)
    col_id = lax.broadcasted_iota(jnp.int32, (BLOCK, BLOCK), 1)
    upper = row_id <= col_id
    eye = (row_id == col_id).astype(jnp.float32)

    def factor_block(kb):
        base = pl.multiple_of(kb * BLOCK, BLOCK)
        for m in range(3):
            work[m, :, :BLOCK] = mats[m, pl.ds(base, BLOCK), pl.ds(base, BLOCK)]
            work[m, :, BLOCK:] = eye
        for p in range(BLOCK // 8):
            lo = 8 * p
            for m in range(3):
                panel = work[m, lo : lo + 8, :]
                for i in range(8):
                    column = panel[:, lo + i : lo + i + 1]
                    root = lax.rsqrt(column[i : i + 1, :])
                    row = panel[i : i + 1, :] * root
                    factor = column * root
                    panel = jnp.where(
                        sub > i, panel - factor * row, jnp.where(sub == i, row, panel)
                    )
                work[m, lo : lo + 8, :] = panel
                if lo + 8 < BLOCK:
                    rest = panel[:, :BLOCK]
                    done = lo + 8
                    rest = jnp.where(lane >= done, rest, 0.0)
                    work[m] = work[m] - dot(rest, panel, 0, 0)
        for m in range(3):
            mats[m, pl.ds(base, BLOCK), pl.ds(base, BLOCK)] = jnp.where(
                upper, work[m, :, :BLOCK], 0.0
            )
            inv[m, pl.ds(base, BLOCK), pl.ds(base, BLOCK)] = jnp.where(
                row_id >= col_id, work[m, :, BLOCK:], 0.0
            )

    def step(kb, carry):
        factor_block(kb)
        for s in range(4):

            @pl.when(kb == s)
            def _():
                lo, hi = s * BLOCK, (s + 1) * BLOCK
                for m in range(3):
                    corner_inv = inv[m, lo:hi, lo:hi]
                    if s > 0:
                        inv[m, lo:hi, :lo] = dot(corner_inv, inv[m, lo:hi, :lo])
                    if s < 3:
                        panel = dot(corner_inv, mats[m, lo:hi, hi:])
                        mats[m, lo:hi, hi:] = panel
                        mats[m, hi:, hi:] = mats[m, hi:, hi:] - dot(panel, panel, 0, 0)
                        inv[m, hi:, :hi] = inv[m, hi:, :hi] - dot(panel, inv[m, lo:hi, :hi], 0, 0)

        return carry

    lax.fori_loop(0, 4, step, 0)
    for s in range(1, 4):
        mats[0, s * BLOCK : (s + 1) * BLOCK, : s * BLOCK] = jnp.zeros(
            (BLOCK, s * BLOCK), jnp.float32
        )

    second[...] = dot(basis[...], inv[0, 256:, :256], 1, 1) + dot(
        krylov[...], inv[0, 256:, 256:], 1, 1
    )
    for k in range(2):
        low = inv[k + 1]
        power = dot(dot(low, cap_mat[...] * ratios[k]), low, 1, 1)
        states = dot(forcing[...] * gains[k], low, 0, 1)
        time = lax.broadcasted_iota(jnp.int32, (STEPS, 512), 0)
        s = 1
        while s < STEPS:
            late = jnp.where(time >= s, pltpu.roll(states, s, 0), 0.0)
            states = states + dot(late, power)
            s *= 2
            if s < STEPS:
                power = dot(power, power)
        response[k] = dot(dot(states, low), mats[0], 1, 1)


def solve(nodes, drivers, sums, basis, krylov, corners, levels):
    vmem = pl.BlockSpec(memory_space=pltpu.VMEM)
    smem = pl.BlockSpec(memory_space=pltpu.SMEM)
    f32 = jnp.float32
    return pl.pallas_call(
        functools.partial(solve_kernel, nodes, drivers),
        out_shape=(
            jax.ShapeDtypeStruct((NODES, K), f32),
            jax.ShapeDtypeStruct((2, STEPS, 2 * K), f32),
        ),
        in_specs=[vmem, vmem, vmem, smem, smem],
        out_specs=(vmem, vmem),
        scratch_shapes=[
            pltpu.VMEM((3, 512, 512), f32),
            pltpu.VMEM((3, 512, 512), f32),
            pltpu.VMEM((512, 512), f32),
            pltpu.VMEM((512, STEPS), f32),
            pltpu.VMEM((3, BLOCK, 2 * BLOCK), f32),
        ],
        compiler_params=pltpu.CompilerParams(vmem_limit_bytes=48 * 1024 * 1024),
        name="solve",
    )(sums, basis, krylov, corners, levels)


def shards(basis_start, admit, pattern, ground, capacity, ports, drive, corner_table, level_table):
    devices = lax.axis_size("gx") * lax.axis_size("gy")
    basis = basis_start.reshape(NODES, K)
    krylov, sums = stats(basis, admit, pattern, ground, capacity, ports, drive)
    second, response = solve(
        NODES * devices, ports.shape[0] * devices, sums, basis, krylov, corner_table, level_table
    )
    return second.reshape(TX, TY, K), response


def solution(mesh):
    return jax.shard_map(
        shards,
        mesh=mesh,
        in_specs=(
            P("gx", "gy", None),
            P("gx", "gy"),
            P("gx", "gy"),
            P("gx", "gy"),
            P("gx", "gy"),
            P(("gx", "gy")),
            P(("gx", "gy"), None),
            P("gy", None),
            P(),
        ),
        out_specs=(P("gx", "gy", None), P("gy", None, None)),
        check_vma=False,
    )
```

```python
import functools
import math

import jax
import jax.numpy as jnp
from jax import lax
from jax.experimental import pallas as pl
from jax.experimental.pallas import tpu as pltpu
from jax.sharding import PartitionSpec as P

MESH = pl.DeviceIdType.MESH
highest = lax.Precision.HIGHEST
time_step = 0.25
K = 256
TX = 8
TY = 128
NODES = TX * TY
STEPS = 64
BLOCK = 128
ROWS = 4096


def dot(a, b, ca=1, cb=0, precision=highest):
    return lax.dot_general(
        a, b, (((ca,), (cb,)), ((), ())), precision=precision, preferred_element_type=jnp.float32
    )


def place():
    gx, gy = lax.axis_index("gx"), lax.axis_index("gy")
    z = (gx // 4) * 2 + (gy % 4) // 2
    return gx, gy, gx % 4, gy // 4, z, gy % 2


def device(x, y, z, core):
    return ((z // 2) * 4 + x, y * 4 + (z % 2) * 2 + core)


def stats_kernel(
    basis, admit, pattern, ground, capacity, ports, drive,
    y_out, out,
    strength, sx, left_send, right_send, tiles, halo_row, halo_col,
    top_send, edge_send, next_row, next_col,
    v, got0, got1, got2, got3, send_sem, recv_sem,
):
    gx, gy, x, y, z, core = place()
    up = (lax.rem(gx + 15, 16), gy)
    down = (lax.rem(gx + 1, 16), gy)
    left = (gx, lax.rem(gy + 15, 16))
    right = (gx, lax.rem(gy + 1, 16))
    sibling = device(x, y, z, 1 - core)
    along_x = [device(lax.rem(x + d, 4), y, z, core) for d in range(1, 4)]
    along_y = [device(x, lax.rem(y + d, 4), z, core) for d in range(1, 4)]
    along_z = [device(x, y, lax.rem(z + d, 8), core) for d in range(1, 8)]
    barrier = pltpu.get_barrier_semaphore()
    partners = [up, down, left, right, sibling] + along_x + along_y + along_z
    for partner in partners:
        pl.semaphore_signal(barrier, inc=1, device_id=partner, device_id_type=MESH)

    started = []

    def send(src, dst, target):
        i = len(started)
        copy = pltpu.make_async_remote_copy(
            src_ref=src, dst_ref=dst, send_sem=send_sem.at[i], recv_sem=recv_sem.at[i],
            device_id=target, device_id_type=MESH,
        )
        copy.start()
        started.append(copy)
        return copy

    strength[...] = admit[...] * pattern[...].astype(jnp.float32)
    own = strength[...]
    own_t = own.T
    for r in range(TX):
        rows = pl.ds(r * TY, TY)
        weighted = own_t[:, r : r + 1] * basis[rows, :]
        sx[rows, :] = weighted
        left_send[r : r + 1, :] = weighted[0:1, :]
        right_send[r : r + 1, :] = weighted[TY - 1 : TY, :]
    pl.semaphore_wait(barrier, len(partners))
    last = (TX - 1) * TY
    halo = [
        send(strength, tiles.at[0], down),
        send(strength, tiles.at[1], up),
        send(strength, tiles.at[2], right),
        send(strength, tiles.at[3], left),
        send(sx.at[pl.ds(last, TY), :], halo_row.at[0], down),
        send(sx.at[pl.ds(0, TY), :], halo_row.at[1], up),
        send(right_send, halo_col.at[0], right),
        send(left_send, halo_col.at[1], left),
    ]

    def put(m, value):
        v[pl.ds(m * 512, 256), :] = value[:, :128]
        v[pl.ds(m * 512 + 256, 256), :] = value[:, 128:]

    xt = basis[...].T
    cap = capacity[...]
    cap_t = cap.T
    for r in range(TX):
        rows = pl.ds(r * TY, TY)
        y_out[rows, :] = cap_t[:, r : r + 1] * basis[rows, :]
    put(0, dot(xt, basis[...]))
    put(3, dot(xt, y_out[...]))

    for copy in halo:
        copy.wait_recv()
    has_up, has_down = gx > 0, gx < 15
    has_left, has_right = gy > 0, gy < 15
    above = jnp.where(has_up, tiles[0, TX - 1 : TX, :], 0.0)
    below = jnp.where(has_down, tiles[1, 0:1, :], 0.0)
    before = jnp.where(has_left, tiles[2, :, TY - 1 : TY], 0.0)
    after = jnp.where(has_right, tiles[3, :, 0:1], 0.0)
    degree = (
        jnp.concatenate([above, own[:-1]], 0)
        + jnp.concatenate([own[1:], below], 0)
        + jnp.concatenate([before, own[:, :-1]], 1)
        + jnp.concatenate([own[:, 1:], after], 1)
    )
    diagonal = ground[...] + own * degree
    diagonal_t = diagonal.T
    place_in_row = lax.broadcasted_iota(jnp.int32, (TY, K), 0)

    def moved_back(block, edge):
        return jnp.where(place_in_row == TY - 1, edge, pltpu.roll(block, TY - 1, 0))

    def moved_on(block, edge):
        return jnp.where(place_in_row == 0, edge, pltpu.roll(block, 1, 0))

    halo_up = jnp.where(has_up, halo_row[0], 0.0)
    halo_down = jnp.where(has_down, halo_row[1], 0.0)
    halo_left = jnp.where(has_left, halo_col[0], 0.0)
    halo_right = jnp.where(has_right, halo_col[1], 0.0)
    for r in range(TX):
        rows = pl.ds(r * TY, TY)
        here = sx[rows, :]
        total = moved_on(here, halo_left[r : r + 1]) + moved_back(here, halo_right[r : r + 1])
        total = total + (halo_up if r == 0 else sx[pl.ds((r - 1) * TY, TY), :])
        total = total + (halo_down if r == TX - 1 else sx[pl.ds((r + 1) * TY, TY), :])
        image = diagonal_t[:, r : r + 1] * basis[rows, :] - own_t[:, r : r + 1] * total
        krylov = image / cap_t[:, r : r + 1]
        y_out[rows, :] = krylov
        weighted = own_t[:, r : r + 1] * krylov
        if r == 0:
            top_send[...] = weighted
        edge_send[r : r + 1, :] = weighted[0:1, :]
    border = [send(top_send, next_row, up), send(edge_send, next_col, left)]

    put(1, dot(xt, y_out[...]))
    yt = y_out[...].T
    put(2, dot(yt, y_out[...]))
    cap_y = jnp.concatenate(
        [cap_t[:, r : r + 1] * y_out[pl.ds(r * TY, TY), :] for r in range(TX)], 0
    )
    put(4, dot(xt, cap_y))
    put(5, dot(yt, cap_y))
    node = lax.broadcasted_iota(jnp.int32, (8, NODES), 1)
    driver = lax.broadcasted_iota(jnp.int32, (8, NODES), 0)
    spot = jnp.full((8, NODES), -1, jnp.int32)
    for d in range(8):
        spot = jnp.where(driver == d, ports[d], spot)
    picked = (node == spot).astype(jnp.float32)
    v[pl.ds(3584, 256), 0:STEPS] = dot(dot(picked, basis[...]), drive[...], 0, 0)
    v[pl.ds(3584, 256), STEPS:128] = dot(dot(picked, y_out[...]), drive[...], 0, 0)
    v[pl.ds(3840, 256), :] = jnp.zeros((256, 128), jnp.float32)

    for copy in border:
        copy.wait_recv()
    bottom = jnp.where(has_down, next_row[...], 0.0)
    side = jnp.where(has_right, next_col[...], 0.0)
    for copy in halo:
        copy.wait_send()
    for r in range(TX):
        rows = pl.ds(r * TY, TY)
        here = own_t[:, r : r + 1] * y_out[rows, :]
        sx[rows, :] = here
    for r in range(TX):
        rows = pl.ds(r * TY, TY)
        total = moved_back(sx[rows, :], side[r : r + 1])
        total = total + (bottom if r == TX - 1 else sx[pl.ds((r + 1) * TY, TY), :])
        sx[rows, :] = (
            0.5 * diagonal_t[:, r : r + 1] * y_out[rows, :] - own_t[:, r : r + 1] * total
        )
    put(6, dot(yt, sx[...]))

    mine = core * 2048
    other = (1 - core) * 2048
    a0, b0 = mine, mine + 1024
    a1, b1 = a0 + x * 256, b0 + y * 256
    a2, b2 = a1 + y * 64, b1 + x * 64
    a3, b3 = a2 + z * 8, b2 + z * 8

    def span(ref, start, size):
        return ref.at[pl.ds(pl.multiple_of(start, 8), size), :]

    first = [
        send(span(v, other + h * 1024, 1024), got0.at[h], sibling) for h in range(2)
    ]

    def spread(base, size, line, position, got, ring):
        return [
            send(span(v, base + lax.rem(position + d, ring) * size, size), got.at[d - 1], line[d - 1])
            for d in range(1, ring)
        ]

    def collect(copies, base, size, got, count):
        for copy in copies:
            copy.wait_recv()
        rows = pl.ds(pl.multiple_of(base, 8), size)
        total = v[rows, :]
        for i in range(count):
            total = total + got[i]
        return total

    for h, base in enumerate((a0, b0)):
        first[h].wait_recv()
        rows = pl.ds(pl.multiple_of(base, 8), 1024)
        v[rows, :] = v[rows, :] + got0[h]
        if h == 0:
            one_a = spread(a0, 256, along_x, x, got1.at[0], 4)
        else:
            one_b = spread(b0, 256, along_y, y, got1.at[1], 4)
    v[pl.ds(pl.multiple_of(a1, 8), 256), :] = collect(one_a, a1, 256, got1.at[0], 3)
    two_a = spread(a1, 64, along_y, y, got2.at[0], 4)
    v[pl.ds(pl.multiple_of(b1, 8), 256), :] = collect(one_b, b1, 256, got1.at[1], 3)
    two_b = spread(b1, 64, along_x, x, got2.at[1], 4)
    v[pl.ds(pl.multiple_of(a2, 8), 64), :] = collect(two_a, a2, 64, got2.at[0], 3)
    three_a = spread(a2, 8, along_z, z, got3.at[0], 8)
    v[pl.ds(pl.multiple_of(b2, 8), 64), :] = collect(two_b, b2, 64, got2.at[1], 3)
    three_b = spread(b2, 8, along_z, z, got3.at[1], 8)

    def share(base, size, line):
        return [send(span(out, base, size), span(out, base, size), target) for target in line]

    out[pl.ds(pl.multiple_of(a3, 8), 8), :] = collect(three_a, a3, 8, got3.at[0], 7)
    back_a = share(a3, 8, along_z)
    out[pl.ds(pl.multiple_of(b3, 8), 8), :] = collect(three_b, b3, 8, got3.at[1], 7)
    back_b = share(b3, 8, along_z)
    for copy in back_a:
        copy.wait_recv()
    back_a = share(a2, 64, along_y)
    for copy in back_b:
        copy.wait_recv()
    back_b = share(b2, 64, along_x)
    for copy in back_a:
        copy.wait_recv()
    back_a = share(a1, 256, along_x)
    for copy in back_b:
        copy.wait_recv()
    back_b = share(b1, 256, along_y)
    for copy in back_a:
        copy.wait_recv()
    back_a = share(a0, 1024, [sibling])
    for copy in back_b:
        copy.wait_recv()
    back_b = share(b0, 1024, [sibling])
    for copy in back_a + back_b:
        copy.wait_recv()
    for copy in started[len(halo) :]:
        copy.wait_send()


def stats(basis, admit, pattern, ground, capacity, ports, drive):
    vmem = pl.BlockSpec(memory_space=pltpu.VMEM)
    smem = pl.BlockSpec(memory_space=pltpu.SMEM)
    f32 = jnp.float32
    copies = 8 + 2 + 2 * (2 + 6 + 6 + 14)
    return pl.pallas_call(
        stats_kernel,
        out_shape=(
            jax.ShapeDtypeStruct((NODES, K), f32),
            jax.ShapeDtypeStruct((ROWS, 128), f32),
        ),
        in_specs=[vmem] * 5 + [smem, vmem],
        out_specs=(vmem, vmem),
        scratch_shapes=[
            pltpu.VMEM((TX, TY), f32),
            pltpu.VMEM((NODES, K), f32),
            pltpu.VMEM((TX, K), f32),
            pltpu.VMEM((TX, K), f32),
            pltpu.VMEM((4, TX, TY), f32),
            pltpu.VMEM((2, TY, K), f32),
            pltpu.VMEM((2, TX, K), f32),
            pltpu.VMEM((TY, K), f32),
            pltpu.VMEM((TX, K), f32),
            pltpu.VMEM((TY, K), f32),
            pltpu.VMEM((TX, K), f32),
            pltpu.VMEM((ROWS, 128), f32),
            pltpu.VMEM((2, 1024, 128), f32),
            pltpu.VMEM((2, 3, 256, 128), f32),
            pltpu.VMEM((2, 3, 64, 128), f32),
            pltpu.VMEM((2, 7, 8, 128), f32),
            pltpu.SemaphoreType.DMA((copies,)),
            pltpu.SemaphoreType.DMA((copies,)),
        ],
        compiler_params=pltpu.CompilerParams(
            collective_id=0, has_side_effects=True, vmem_limit_bytes=48 * 1024 * 1024
        ),
        name="stats",
    )(basis, admit, pattern, ground, capacity, ports, drive)


def split(a, count):
    parts = []
    for _ in range(count - 1):
        part = a.astype(jnp.bfloat16)
        parts.append(part)
        a = a - part.astype(jnp.float32)
    return parts + [a.astype(jnp.bfloat16)]


PAIRS = {2: ((0, 0), (0, 1), (1, 0)), 3: ((0, 0), (0, 1), (1, 0), (1, 1), (0, 2), (2, 0))}


def deep_dot(a, b, ca, cb, count=3):
    pairs = PAIRS[count]
    left = jnp.concatenate([a[i] for i, j in pairs], ca)
    right = jnp.concatenate([b[j] for i, j in pairs], cb)
    return lax.dot_general(
        left, right, (((ca,), (cb,)), ((), ())), preferred_element_type=jnp.float32
    )


def sum_dot(a, b, ca=1, cb=0, count=2):
    total = None
    for i, j in PAIRS[count]:
        term = lax.dot_general(
            a[i], b[j], (((ca,), (cb,)), ((), ())), preferred_element_type=jnp.float32
        )
        total = term if total is None else total + term
    return total


def solve_kernel(
    nodes, drivers, sums, corners, levels, next_map, response,
    mats, low_t, cap_mat, forcing, work,
):
    scale = 1.0 / nodes

    def take(m):
        return (
            jnp.concatenate([sums[pl.ds(m * 512, 256), :], sums[pl.ds(m * 512 + 256, 256), :]], 1)
            * scale
        )

    xx, xy, yy, xcx, xcy, ycy, half = [take(m) for m in range(7)]
    mats[0, :256, :256] = xx
    mats[0, :256, 256:] = xy
    mats[0, 256:, 256:] = yy
    cap_mat[:256, :256] = xcx
    cap_mat[:256, 256:] = xcy
    cap_mat[256:, :256] = xcy.T
    cap_mat[256:, 256:] = ycy
    cond_tail = half + half.T
    k = lax.rem(lax.axis_index("gx"), 2)
    g = levels[0, corners[k, 0]]
    ratio = levels[1, corners[k, 1]] * (1.0 / time_step)
    gain = levels[2, corners[k, 2]]
    mats[1, :256, :256] = g * xcy + ratio * xcx
    mats[1, :256, 256:] = g * ycy + ratio * xcy
    mats[1, 256:, 256:] = g * cond_tail + ratio * ycy
    part = sums[pl.ds(3584, 256), :] * (1.0 / math.sqrt(drivers))
    forcing[:256, :] = part[:, :STEPS]
    forcing[256:, :] = part[:, STEPS:]
    for m in range(2):
        mats[m, 256:, :256] = jnp.zeros((256, 256), jnp.float32)

    sub = lax.broadcasted_iota(jnp.int32, (8, 128), 0)
    row_id = lax.broadcasted_iota(jnp.int32, (BLOCK, BLOCK), 0)
    col_id = lax.broadcasted_iota(jnp.int32, (BLOCK, BLOCK), 1)
    eye = (row_id == col_id).astype(jnp.float32)

    def factor_panel(lo):
        rows = [[[work[m, lo + 8 * t : lo + 8 * t + 8, h * 128 : h * 128 + 128] for h in range(2)]
                 for t in range(2)] for m in range(2)]
        cols = [[[jnp.broadcast_to(rows[m][t][0][:, lo + k : lo + k + 1], (8, 128))
                  for k in range(16)] for t in range(2)] for m in range(2)]
        pivots = [[None, None] for m in range(2)]
        for i in range(16):
            own, at = i // 8, i % 8
            for m in range(2):
                col, row = cols[m], rows[m]
                pivot = jnp.broadcast_to(col[own][i][at : at + 1, :], (8, 128))
                inverse = 1.0 / pivot
                saved = pivots[m][own]
                pivots[m][own] = pivot if saved is None else jnp.where(sub == at, pivot, saved)
                below = [
                    jnp.where(sub > at, col[t][i], 0.0) if t == own else col[t][i] for t in range(2)
                ]
                for k in range(i + 1, 16):
                    top = jnp.broadcast_to(col[own][k][at : at + 1, :], (8, 128))
                    for t in range(own, 2):
                        col[t][k] = col[t][k] - (below[t] * top) * inverse
                for h in range(2):
                    top = jnp.broadcast_to(row[own][h][at : at + 1, :], (8, 128))
                    for t in range(own, 2):
                        row[t][h] = row[t][h] - (below[t] * top) * inverse
        done = lo + 16
        for m in range(2):
            root = [lax.rsqrt(pivots[m][t]) for t in range(2)]
            panel = jnp.concatenate(
                [jnp.concatenate([rows[m][t][h] * root[t] for h in range(2)], 1) for t in range(2)],
                0,
            )
            work[m, lo:done, :] = panel
            if done < BLOCK:
                parts = split(panel, 3)
                update = deep_dot([p[:, :BLOCK] for p in parts], parts, 0, 0)
                work[m, done:, :] = work[m, done:, :] - update[done:, :]

    def step(s, carry):
        lo = pl.multiple_of(s * BLOCK, BLOCK)
        for m in range(2):
            work[m, :, :BLOCK] = mats[m, pl.ds(lo, BLOCK), pl.ds(lo, BLOCK)]
            work[m, :, BLOCK:] = eye
        for p in range(BLOCK // 16):
            factor_panel(16 * p)
        low_t[pl.ds(lo, BLOCK), pl.ds(lo, BLOCK)] = jnp.where(
            row_id <= col_id, work[0, :, :BLOCK], 0.0
        )
        for i in range(4):

            @pl.when(s == i)
            def _():
                lo, hi = i * BLOCK, (i + 1) * BLOCK
                for m in range(2):
                    corner = jnp.where(row_id >= col_id, work[m, :, BLOCK:], 0.0)
                    row = deep_dot(split(corner, 3), split(mats[m, lo:hi, :], 3), 1, 0)
                    if i > 0:
                        mats[m, lo:hi, :lo] = row[:, :lo]
                    mats[m, lo:hi, lo:hi] = corner
                    if i < 3:
                        mats[m, lo:hi, hi:] = jnp.zeros((BLOCK, 512 - hi), jnp.float32)
                        if m == 0:
                            low_t[lo:hi, hi:] = row[:, hi:]
                        left = [row[:, :lo]] if i > 0 else []
                        row = jnp.concatenate(left + [corner, row[:, hi:]], 1)
                        parts = split(row, 3)
                        update = deep_dot([p[:, hi:] for p in parts], parts, 0, 0)
                        if i > 0:
                            mats[m, hi:, :lo] = mats[m, hi:, :lo] - update[:, :lo]
                        mats[m, hi:, lo:hi] = -update[:, lo:hi]
                        mats[m, hi:, hi:] = mats[m, hi:, hi:] - update[:, hi:]

        return carry

    low_t[...] = jnp.zeros_like(low_t)
    lax.fori_loop(0, 4, step, 0)

    next_map[...] = mats[0, 256:, :]
    low = split(mats[1], 3)
    half_way = sum_dot(low, split(cap_mat[...] * ratio, 3), 1, 0, 3)
    power = sum_dot(split(half_way, 3), low, 1, 1, 3)
    states = sum_dot(split(forcing[...] * gain, 3), low, 0, 1, 3)
    time = lax.broadcasted_iota(jnp.int32, (STEPS, 512), 0)
    s = 1
    while s < STEPS:
        late = jnp.where(time >= s, pltpu.roll(states, s, 0), 0.0)
        parts = split(power, 2)
        states = states + sum_dot(split(late, 2), parts)
        if 2 * s < STEPS:
            power = sum_dot(parts, parts)
        s *= 2
    states = sum_dot(split(states, 3), low, 1, 0, 3)
    response[...] = sum_dot(split(states, 3), split(low_t[...], 3), 1, 1, 3)


def solve(nodes, drivers, sums, corners, levels):
    vmem = pl.BlockSpec(memory_space=pltpu.VMEM)
    smem = pl.BlockSpec(memory_space=pltpu.SMEM)
    f32 = jnp.float32
    return pl.pallas_call(
        functools.partial(solve_kernel, nodes, drivers),
        out_shape=(
            jax.ShapeDtypeStruct((K, 2 * K), f32),
            jax.ShapeDtypeStruct((STEPS, 2 * K), f32),
        ),
        in_specs=[vmem, smem, smem],
        out_specs=(vmem, vmem),
        scratch_shapes=[
            pltpu.VMEM((2, 512, 512), f32),
            pltpu.VMEM((512, 512), f32),
            pltpu.VMEM((512, 512), f32),
            pltpu.VMEM((512, STEPS), f32),
            pltpu.VMEM((2, BLOCK, 2 * BLOCK), f32),
        ],
        compiler_params=pltpu.CompilerParams(vmem_limit_bytes=48 * 1024 * 1024),
        name="solve",
    )(sums, corners, levels)


def project_kernel(basis, krylov, next_map, second):
    maps = split(next_map[...], 2)
    for c in range(4):
        rows = pl.ds(c * 256, 256)
        second[rows, :] = sum_dot(
            split(basis[rows, :], 2), [m[:, :256] for m in maps], 1, 1
        ) + sum_dot(split(krylov[rows, :], 2), [m[:, 256:] for m in maps], 1, 1)


def project(basis, krylov, next_map):
    vmem = pl.BlockSpec(memory_space=pltpu.VMEM)
    return pl.pallas_call(
        project_kernel,
        out_shape=jax.ShapeDtypeStruct((NODES, K), jnp.float32),
        in_specs=[vmem, vmem, vmem],
        out_specs=vmem,
        compiler_params=pltpu.CompilerParams(vmem_limit_bytes=32 * 1024 * 1024),
        cost_estimate=pl.CostEstimate(
            flops=2 * NODES * 2 * K * K * 3, bytes_accessed=4 * 2**20, transcendentals=0
        ),
        name="project",
    )(basis, krylov, next_map)


def shards(basis_start, admit, pattern, ground, capacity, ports, drive, corner_table, level_table):
    devices = lax.axis_size("gx") * lax.axis_size("gy")
    basis = basis_start.reshape(NODES, K)
    krylov, sums = stats(basis, admit, pattern, ground, capacity, ports, drive)
    next_map, own = solve(
        NODES * devices, ports.shape[0] * devices, sums, corner_table, level_table
    )
    swap = [(i, i ^ 1) for i in range(lax.axis_size("gx"))]
    other = lax.ppermute(own, "gx", swap)
    second = project(basis, krylov, next_map)
    even = lax.rem(lax.axis_index("gx"), 2) == 0
    response = jnp.stack([jnp.where(even, own, other), jnp.where(even, other, own)])
    return second.reshape(TX, TY, K), response


def solution(mesh):
    return jax.shard_map(
        shards,
        mesh=mesh,
        in_specs=(
            P("gx", "gy", None),
            P("gx", "gy"),
            P("gx", "gy"),
            P("gx", "gy"),
            P("gx", "gy"),
            P(("gx", "gy")),
            P(("gx", "gy"), None),
            P("gy", None),
            P(),
        ),
        out_specs=(P("gx", "gy", None), P("gy", None, None)),
        check_vma=False,
    )
```

```python
import functools
import math

import jax
import jax.numpy as jnp
from jax import lax
from jax.experimental import pallas as pl
from jax.experimental.pallas import tpu as pltpu
from jax.sharding import PartitionSpec as P

MESH = pl.DeviceIdType.MESH
highest = lax.Precision.HIGHEST
time_step = 0.25
K = 256
TX = 8
TY = 128
NODES = TX * TY
STEPS = 64
BLOCK = 128


def dot(a, b, ca=1, cb=0, precision=highest):
    return lax.dot_general(
        a, b, (((ca,), (cb,)), ((), ())), precision=precision, preferred_element_type=jnp.float32
    )


def place():
    gx, gy = lax.axis_index("gx"), lax.axis_index("gy")
    z = (gx // 4) * 2 + (gy % 4) // 2
    return gx, gy, gx % 4, gy // 4, z, gy % 2


def device(x, y, z, core):
    return ((z // 2) * 4 + x, y * 4 + (z % 2) * 2 + core)


WAVES = 5
WAVE = 512
HALF = 256
PIECE = 16
SCALES = 3 * WAVE + 264


def stats_kernel(
    basis_in, admit_in, pattern_in, ground_in, capacity_in, ports_in, drive_in,
    corners_in, levels_in, y_copy, out,
    basis, admit, pattern, ground, capacity, ports, drive, corners, levels, load_sem,
    y_out, y_sem,
    strength, sx, left_send, right_send, tiles, halo_row, halo_col,
    top_send, edge_send, next_row, next_col,
    v, got_core, got_plane, got_z, send_sem, recv_sem,
):
    gx, gy, x, y, z, core = place()
    up = (lax.rem(gx + 15, 16), gy)
    down = (lax.rem(gx + 1, 16), gy)
    left = (gx, lax.rem(gy + 15, 16))
    right = (gx, lax.rem(gy + 1, 16))
    sibling = device(x, y, z, 1 - core)
    plane = []
    for d in range(1, 16):
        px, py = lax.rem(x + d % 4, 4), lax.rem(y + d // 4, 4)
        plane.append((px * 4 + py, device(px, py, z, core)))
    along_z = [device(x, y, lax.rem(z + d, 8), core) for d in range(1, 8)]
    barrier = pltpu.get_barrier_semaphore()
    partners = [up, down, left, right, sibling] + [p[1] for p in plane] + along_z
    for partner in partners:
        pl.semaphore_signal(barrier, inc=1, device_id=partner, device_id_type=MESH)
    loads = [
        pltpu.make_async_copy(src, dst, load_sem.at[i])
        for i, (src, dst) in enumerate(
            (
                (basis_in, basis), (admit_in, admit), (pattern_in, pattern), (ground_in, ground),
                (capacity_in, capacity), (ports_in, ports), (drive_in, drive),
                (corners_in, corners), (levels_in, levels),
            )
        )
    ]
    for copy in loads:
        copy.start()

    started = []

    def send(src, dst, target):
        i = len(started)
        copy = pltpu.make_async_remote_copy(
            src_ref=src, dst_ref=dst, send_sem=send_sem.at[i], recv_sem=recv_sem.at[i],
            device_id=target, device_id_type=MESH,
        )
        copy.start()
        started.append(copy)
        return copy

    home = x * 4 + y
    flights = {}

    def span(ref, start, size):
        return ref.at[pl.ds(pl.multiple_of(start, 8), size), :]

    def start_core(w):
        start = w * WAVE + (1 - core) * HALF
        flights[w] = [send(span(v, start, HALF), got_core.at[w], sibling)]

    def landed(w):
        for copy in flights[w]:
            copy.wait_recv()

    def start_plane(w):
        landed(w)
        start = w * WAVE + core * HALF
        rows = pl.ds(pl.multiple_of(start, 8), HALF)
        v[rows, :] = v[rows, :] + got_core[w]
        flights[w] = [
            send(span(v, start + spot * PIECE, PIECE), got_plane.at[w, i], target)
            for i, (spot, target) in enumerate(plane)
        ]

    def start_z(w):
        landed(w)
        start = w * WAVE + core * HALF + home * PIECE
        total = v[pl.ds(pl.multiple_of(start, 8), PIECE), :]
        for i in range(15):
            total = total + got_plane[w, i]
        got_z[w, z] = total
        flights[w] = [send(got_z.at[w, z], got_z.at[w, z], target) for target in along_z]

    def start_back(w):
        landed(w)
        total = got_z[w, 0]
        for i in range(1, 8):
            total = total + got_z[w, i]
        start = w * WAVE + core * HALF + home * PIECE
        out[pl.ds(pl.multiple_of(start, 8), PIECE), :] = total
        flights[w] = [
            send(span(out, start, PIECE), span(out, start, PIECE), target) for _, target in plane
        ]

    def start_last(w):
        landed(w)
        start = w * WAVE + core * HALF
        flights[w] = [send(span(out, start, HALF), span(out, start, HALF), sibling)]

    def put(w, value):
        v[pl.ds(w * WAVE, 256), :] = value[:, :128]
        v[pl.ds(w * WAVE + 256, 256), :] = value[:, 128:]

    row_id = lax.broadcasted_iota(jnp.int32, (K, K), 0)
    col_id = lax.broadcasted_iota(jnp.int32, (K, K), 1)

    def put_pair(w, lower, upper):
        put(w, jnp.where(row_id >= col_id, lower, upper))

    def gram(left_parts, right_parts):
        return sum_dot(left_parts, right_parts, 1, 0, 4)

    for copy in loads:
        copy.wait()
    strength[...] = admit[...] * pattern[...].astype(jnp.float32)
    own = strength[...]
    own_t = own.T
    cap_t = capacity[...].T
    for r in range(TX):
        rows = pl.ds(r * TY, TY)
        weighted = own_t[:, r : r + 1] * basis[rows, :]
        sx[rows, :] = weighted
        left_send[r : r + 1, :] = weighted[0:1, :]
        right_send[r : r + 1, :] = weighted[TY - 1 : TY, :]

    def capped(ref):
        return jnp.concatenate(
            [cap_t[:, r : r + 1] * ref[pl.ds(r * TY, TY), :] for r in range(TX)], 0
        )

    x_parts = split(basis[...], 2)
    xt_parts = split(basis[...].T, 2)
    cap_x = capped(basis)
    put_pair(0, gram(xt_parts, x_parts), gram(xt_parts, split(cap_x, 2)))

    pl.semaphore_wait(barrier, len(partners))
    last = (TX - 1) * TY
    halo = [
        send(strength, tiles.at[0], down),
        send(strength, tiles.at[1], up),
        send(strength, tiles.at[2], right),
        send(strength, tiles.at[3], left),
        send(sx.at[pl.ds(last, TY), :], halo_row.at[0], down),
        send(sx.at[pl.ds(0, TY), :], halo_row.at[1], up),
        send(right_send, halo_col.at[0], right),
        send(left_send, halo_col.at[1], left),
    ]
    start_core(0)
    node = lax.broadcasted_iota(jnp.int32, (8, NODES), 1)
    driver = lax.broadcasted_iota(jnp.int32, (8, NODES), 0)
    spot = jnp.full((8, NODES), -1, jnp.int32)
    for d in range(8):
        spot = jnp.where(driver == d, ports[d], spot)
    picked = (node == spot).astype(jnp.float32)
    v[pl.ds(3 * WAVE, 256), 0:STEPS] = dot(dot(picked, basis[...]), drive[...], 0, 0)
    start_plane(0)

    for copy in halo:
        copy.wait_recv()
    has_up, has_down = gx > 0, gx < 15
    has_left, has_right = gy > 0, gy < 15
    above = jnp.where(has_up, tiles[0, TX - 1 : TX, :], 0.0)
    below = jnp.where(has_down, tiles[1, 0:1, :], 0.0)
    before = jnp.where(has_left, tiles[2, :, TY - 1 : TY], 0.0)
    after = jnp.where(has_right, tiles[3, :, 0:1], 0.0)
    degree = (
        jnp.concatenate([above, own[:-1]], 0)
        + jnp.concatenate([own[1:], below], 0)
        + jnp.concatenate([before, own[:, :-1]], 1)
        + jnp.concatenate([own[:, 1:], after], 1)
    )
    diagonal_t = (ground[...] + own * degree).T
    place_in_row = lax.broadcasted_iota(jnp.int32, (TY, K), 0)

    def moved_back(block, edge):
        return jnp.where(place_in_row == TY - 1, edge, pltpu.roll(block, TY - 1, 0))

    def moved_on(block, edge):
        return jnp.where(place_in_row == 0, edge, pltpu.roll(block, 1, 0))

    halo_up = jnp.where(has_up, halo_row[0], 0.0)
    halo_down = jnp.where(has_down, halo_row[1], 0.0)
    halo_left = jnp.where(has_left, halo_col[0], 0.0)
    halo_right = jnp.where(has_right, halo_col[1], 0.0)
    inverse_t = 1.0 / cap_t
    for r in range(TX):
        rows = pl.ds(r * TY, TY)
        here = sx[rows, :]
        total = moved_on(here, halo_left[r : r + 1]) + moved_back(here, halo_right[r : r + 1])
        total = total + (halo_up if r == 0 else sx[pl.ds((r - 1) * TY, TY), :])
        total = total + (halo_down if r == TX - 1 else sx[pl.ds((r + 1) * TY, TY), :])
        image = diagonal_t[:, r : r + 1] * basis[rows, :] - own_t[:, r : r + 1] * total
        krylov = image * inverse_t[:, r : r + 1]
        y_out[rows, :] = krylov
        weighted = own_t[:, r : r + 1] * krylov
        if r == 0:
            top_send[...] = weighted
        edge_send[r : r + 1, :] = weighted[0:1, :]
    y_store = pltpu.make_async_copy(y_out, y_copy, y_sem)
    y_store.start()
    border = [send(top_send, next_row, up), send(edge_send, next_col, left)]

    y_parts = split(y_out[...], 2)
    put(1, gram(xt_parts, y_parts))
    start_core(1)
    cap_y = capped(y_out)
    v[pl.ds(3 * WAVE, 256), STEPS:128] = dot(dot(picked, y_out[...]), drive[...], 0, 0)
    v[pl.ds(3 * WAVE + 256, 256), :] = jnp.zeros((256, 128), jnp.float32)
    for i, squares in enumerate(
        (basis[...] * cap_x, basis[...] * cap_y, y_out[...] * cap_y)
    ):
        along = jnp.sum(squares, axis=0, keepdims=True)
        v[3 * WAVE + 256 + 2 * i : 3 * WAVE + 257 + 2 * i, :] = along[:, :128]
        v[3 * WAVE + 257 + 2 * i : 3 * WAVE + 258 + 2 * i, :] = along[:, 128:]
    start_core(3)
    start_plane(1)
    yt_parts = split(y_out[...].T, 2)
    cap_parts = split(cap_y, 2)
    cross = gram(xt_parts, cap_parts)
    put_pair(2, gram(yt_parts, y_parts), 0.5 * (cross + cross.T))
    start_core(2)
    start_plane(3)
    start_z(0)
    tail = gram(yt_parts, cap_parts)
    start_plane(2)

    for copy in border:
        copy.wait_recv()
    for copy in halo:
        copy.wait_send()
    bottom = jnp.where(has_down, next_row[...], 0.0)
    side = jnp.where(has_right, next_col[...], 0.0)
    for r in range(TX):
        rows = pl.ds(r * TY, TY)
        sx[rows, :] = own_t[:, r : r + 1] * y_out[rows, :]
    for r in range(TX):
        rows = pl.ds(r * TY, TY)
        total = moved_back(sx[rows, :], side[r : r + 1])
        total = total + (bottom if r == TX - 1 else sx[pl.ds((r + 1) * TY, TY), :])
        sx[rows, :] = (
            0.5 * diagonal_t[:, r : r + 1] * y_out[rows, :] - own_t[:, r : r + 1] * total
        )
    start_z(1)
    half = gram(yt_parts, split(sx[...], 2))
    put_pair(4, half + half.T, tail)
    start_core(4)
    start_back(0)
    start_z(3)
    start_plane(4)
    start_z(2)
    start_back(1)
    start_last(0)
    start_back(3)
    start_back(2)
    start_z(4)
    for w in (1, 3, 2):
        start_last(w)
    start_back(4)
    start_last(4)
    for w in range(WAVES):
        landed(w)
    y_store.wait()
    for copy in started[len(halo) :]:
        copy.wait_send()
    for kind in range(3):
        for k in range(2):
            level = levels[kind, 0]
            for i in range(1, 4):
                level = jnp.where(corners[k, kind] == i, levels[kind, i], level)
            out[SCALES + 2 * kind + k : SCALES + 2 * kind + k + 1, :] = jnp.full((1, 128), level, jnp.float32)


def stats(basis, admit, pattern, ground, capacity, ports, drive, corners, levels):
    vmem = pl.BlockSpec(memory_space=pltpu.VMEM)
    anywhere = pl.BlockSpec(memory_space=pl.ANY)
    f32 = jnp.float32
    copies = 8 + 2 + WAVES * (1 + 15 + 7 + 15 + 1)
    return pl.pallas_call(
        stats_kernel,
        out_shape=(
            jax.ShapeDtypeStruct((NODES, K), f32),
            jax.ShapeDtypeStruct((WAVES * WAVE, 128), f32),
        ),
        in_specs=[anywhere] * 9,
        out_specs=(anywhere, vmem),
        scratch_shapes=[
            pltpu.VMEM((NODES, K), f32),
            pltpu.VMEM((TX, TY), f32),
            pltpu.VMEM((TX, TY), jnp.int32),
            pltpu.VMEM((TX, TY), f32),
            pltpu.VMEM((TX, TY), f32),
            pltpu.SMEM((8,), jnp.int32),
            pltpu.VMEM((8, STEPS), f32),
            pltpu.SMEM((2, 3), jnp.int32),
            pltpu.SMEM((3, 4), f32),
            pltpu.SemaphoreType.DMA((9,)),
            pltpu.VMEM((NODES, K), f32),
            pltpu.SemaphoreType.DMA,
            pltpu.VMEM((TX, TY), f32),
            pltpu.VMEM((NODES, K), f32),
            pltpu.VMEM((TX, K), f32),
            pltpu.VMEM((TX, K), f32),
            pltpu.VMEM((4, TX, TY), f32),
            pltpu.VMEM((2, TY, K), f32),
            pltpu.VMEM((2, TX, K), f32),
            pltpu.VMEM((TY, K), f32),
            pltpu.VMEM((TX, K), f32),
            pltpu.VMEM((TY, K), f32),
            pltpu.VMEM((TX, K), f32),
            pltpu.VMEM((WAVES * WAVE, 128), f32),
            pltpu.VMEM((WAVES, HALF, 128), f32),
            pltpu.VMEM((WAVES, 15, PIECE, 128), f32),
            pltpu.VMEM((WAVES, 8, PIECE, 128), f32),
            pltpu.SemaphoreType.DMA((copies,)),
            pltpu.SemaphoreType.DMA((copies,)),
        ],
        compiler_params=pltpu.CompilerParams(
            collective_id=0, has_side_effects=True, vmem_limit_bytes=65024 * 1024
        ),
        name="stats",
    )(basis, admit, pattern, ground, capacity, ports, drive, corners, levels)


def split(a, count):
    parts = []
    for _ in range(count - 1):
        part = a.astype(jnp.bfloat16)
        parts.append(part)
        a = a - part.astype(jnp.float32)
    return parts + [a.astype(jnp.bfloat16)]


PAIRS = {
    2: ((0, 0), (0, 1), (1, 0)),
    4: ((0, 0), (0, 1), (1, 0), (1, 1)),
    3: ((0, 0), (0, 1), (1, 0), (1, 1), (0, 2), (2, 0)),
}


def deep_dot(a, b, ca, cb, count=3):
    pairs = PAIRS[count]
    left = jnp.concatenate([a[i] for i, j in pairs], ca)
    right = jnp.concatenate([b[j] for i, j in pairs], cb)
    return lax.dot_general(
        left, right, (((ca,), (cb,)), ((), ())), preferred_element_type=jnp.float32
    )


def sum_dot(a, b, ca=1, cb=0, count=2):
    total = None
    for i, j in PAIRS[count]:
        term = lax.dot_general(
            a[i], b[j], (((ca,), (cb,)), ((), ())), preferred_element_type=jnp.float32
        )
        total = term if total is None else total + term
    return total


def solve_kernel(
    nodes, drivers, sums, next_map, response,
    mats, low_t, cap_mat, forcing, work,
):
    scale = 1.0 / nodes

    row_id = lax.broadcasted_iota(jnp.int32, (K, K), 0)
    col_id = lax.broadcasted_iota(jnp.int32, (K, K), 1)

    def take(w):
        start = w * WAVE
        return (
            jnp.concatenate([sums[pl.ds(start, 256), :], sums[pl.ds(start + 256, 256), :]], 1)
            * scale
        )

    def take_pair(w, place):
        both = take(w)
        turned = both.T
        at = 3 * WAVE + 256 + 2 * place
        diag = jnp.concatenate([sums[at : at + 1, :], sums[at + 1 : at + 2, :]], 1) * scale
        lower = jnp.where(row_id >= col_id, both, turned)
        upper = jnp.where(row_id < col_id, both, jnp.where(row_id == col_id, diag, turned))
        return lower, upper

    xx, xcx = take_pair(0, 0)
    xy = take(1)
    yy, xcy = take_pair(2, 1)
    cond_tail, ycy = take_pair(4, 2)
    mats[0, :256, :256] = xx
    mats[0, :256, 256:] = xy
    mats[0, 256:, 256:] = yy
    cap_mat[:256, :256] = xcx
    cap_mat[:256, 256:] = xcy
    cap_mat[256:, :256] = xcy
    cap_mat[256:, 256:] = ycy
    k = lax.rem(lax.axis_index("gx"), 2)
    g, ratio, gain = [
        jnp.where(
            k == 0,
            sums[SCALES + 2 * i : SCALES + 2 * i + 1, 0:1],
            sums[SCALES + 2 * i + 1 : SCALES + 2 * i + 2, 0:1],
        )
        for i in range(3)
    ]
    ratio = ratio * (1.0 / time_step)
    mats[1, :256, :256] = g * xcy + ratio * xcx
    mats[1, :256, 256:] = g * ycy + ratio * xcy
    mats[1, 256:, 256:] = g * cond_tail + ratio * ycy
    part = sums[pl.ds(3 * WAVE, 256), :] * (1.0 / math.sqrt(drivers))
    forcing[:256, :] = part[:, :STEPS]
    forcing[256:, :] = part[:, STEPS:]
    for m in range(2):
        mats[m, 256:, :256] = jnp.zeros((256, 256), jnp.float32)

    sub = lax.broadcasted_iota(jnp.int32, (8, 128), 0)
    row_id = lax.broadcasted_iota(jnp.int32, (BLOCK, BLOCK), 0)
    col_id = lax.broadcasted_iota(jnp.int32, (BLOCK, BLOCK), 1)
    eye = (row_id == col_id).astype(jnp.float32)

    def factor_panel(lo):
        rows = [[[work[m, lo + 8 * t : lo + 8 * t + 8, h * 128 : h * 128 + 128] for h in range(2)]
                 for t in range(2)] for m in range(2)]
        cols = [[[jnp.broadcast_to(rows[m][t][0][:, lo + k : lo + k + 1], (8, 128))
                  for k in range(16)] for t in range(2)] for m in range(2)]
        pivots = [[None, None] for m in range(2)]
        for i in range(16):
            own, at = i // 8, i % 8
            for m in range(2):
                col, row = cols[m], rows[m]
                pivot = jnp.broadcast_to(col[own][i][at : at + 1, :], (8, 128))
                inverse = 1.0 / pivot
                saved = pivots[m][own]
                pivots[m][own] = pivot if saved is None else jnp.where(sub == at, pivot, saved)
                below = [
                    jnp.where(sub > at, col[t][i], 0.0) if t == own else col[t][i] for t in range(2)
                ]
                for k in range(i + 1, 16):
                    top = jnp.broadcast_to(col[own][k][at : at + 1, :], (8, 128))
                    for t in range(own, 2):
                        col[t][k] = col[t][k] - (below[t] * top) * inverse
                for h in range(2):
                    top = jnp.broadcast_to(row[own][h][at : at + 1, :], (8, 128))
                    for t in range(own, 2):
                        row[t][h] = row[t][h] - (below[t] * top) * inverse
        done = lo + 16
        for m in range(2):
            root = [lax.rsqrt(pivots[m][t]) for t in range(2)]
            panel = jnp.concatenate(
                [jnp.concatenate([rows[m][t][h] * root[t] for h in range(2)], 1) for t in range(2)],
                0,
            )
            work[m, lo:done, :] = panel
            if done < BLOCK:
                parts = split(panel, 3)
                update = deep_dot([p[:, :BLOCK] for p in parts], parts, 0, 0)
                work[m, done:, :] = work[m, done:, :] - update[done:, :]

    def step(s, carry):
        lo = pl.multiple_of(s * BLOCK, BLOCK)
        for m in range(2):
            work[m, :, :BLOCK] = mats[m, pl.ds(lo, BLOCK), pl.ds(lo, BLOCK)]
            work[m, :, BLOCK:] = eye
        for p in range(BLOCK // 16):
            factor_panel(16 * p)
        low_t[pl.ds(lo, BLOCK), pl.ds(lo, BLOCK)] = jnp.where(
            row_id <= col_id, work[0, :, :BLOCK], 0.0
        )
        for i in range(4):

            @pl.when(s == i)
            def _():
                lo, hi = i * BLOCK, (i + 1) * BLOCK
                for m in range(2):
                    corner = jnp.where(row_id >= col_id, work[m, :, BLOCK:], 0.0)
                    row = deep_dot(split(corner, 3), split(mats[m, lo:hi, :], 3), 1, 0)
                    if i > 0:
                        mats[m, lo:hi, :lo] = row[:, :lo]
                    mats[m, lo:hi, lo:hi] = corner
                    if i < 3:
                        mats[m, lo:hi, hi:] = jnp.zeros((BLOCK, 512 - hi), jnp.float32)
                        if m == 0:
                            low_t[lo:hi, hi:] = row[:, hi:]
                        left = [row[:, :lo]] if i > 0 else []
                        row = jnp.concatenate(left + [corner, row[:, hi:]], 1)
                        parts = split(row, 3)
                        update = deep_dot([p[:, hi:] for p in parts], parts, 0, 0)
                        if i > 0:
                            mats[m, hi:, :lo] = mats[m, hi:, :lo] - update[:, :lo]
                        mats[m, hi:, lo:hi] = -update[:, lo:hi]
                        mats[m, hi:, hi:] = mats[m, hi:, hi:] - update[:, hi:]

        return carry

    low_t[...] = jnp.zeros_like(low_t)
    lax.fori_loop(0, 4, step, 0)

    next_map[...] = mats[0, 256:, :]
    low = split(mats[1], 3)
    half_way = sum_dot(low, split(cap_mat[...] * ratio, 3), 1, 0, 3)
    power = sum_dot(split(half_way, 3), low, 1, 1, 3)
    states = sum_dot(split(forcing[...] * gain, 3), low, 0, 1, 3)
    time = lax.broadcasted_iota(jnp.int32, (STEPS, 512), 0)
    s = 1
    while s < STEPS:
        late = jnp.where(time >= s, pltpu.roll(states, s, 0), 0.0)
        parts = split(power, 2)
        late_parts = split(late, 2)
        if 2 * s < STEPS:
            both = sum_dot(
                [jnp.concatenate([p, q], 0) for p, q in zip(parts, late_parts)], parts
            )
            power = both[:512]
            states = states + both[512:]
        else:
            states = states + sum_dot(late_parts, parts)
        s *= 2
    states = sum_dot(split(states, 3), low, 1, 0, 3)
    response[...] = sum_dot(split(states, 3), split(low_t[...], 3), 1, 1, 3)


def solve(nodes, drivers, sums):
    vmem = pl.BlockSpec(memory_space=pltpu.VMEM)
    f32 = jnp.float32
    return pl.pallas_call(
        functools.partial(solve_kernel, nodes, drivers),
        out_shape=(
            jax.ShapeDtypeStruct((K, 2 * K), f32),
            jax.ShapeDtypeStruct((STEPS, 2 * K), f32),
        ),
        in_specs=[vmem],
        out_specs=(vmem, vmem),
        scratch_shapes=[
            pltpu.VMEM((2, 512, 512), f32),
            pltpu.VMEM((512, 512), f32),
            pltpu.VMEM((512, 512), f32),
            pltpu.VMEM((512, STEPS), f32),
            pltpu.VMEM((2, BLOCK, 2 * BLOCK), f32),
        ],
        compiler_params=pltpu.CompilerParams(vmem_limit_bytes=48 * 1024 * 1024),
        name="solve",
    )(sums)


def project_kernel(basis, krylov, next_map, second):
    maps = split(next_map[...], 2)
    for c in range(4):
        rows = pl.ds(c * 256, 256)
        second[rows, :] = sum_dot(
            split(basis[rows, :], 2), [m[:, :256] for m in maps], 1, 1
        ) + sum_dot(split(krylov[rows, :], 2), [m[:, 256:] for m in maps], 1, 1)


def project(basis, krylov, next_map):
    vmem = pl.BlockSpec(memory_space=pltpu.VMEM)
    return pl.pallas_call(
        project_kernel,
        out_shape=jax.ShapeDtypeStruct((NODES, K), jnp.float32),
        in_specs=[vmem, vmem, vmem],
        out_specs=vmem,
        compiler_params=pltpu.CompilerParams(vmem_limit_bytes=32 * 1024 * 1024),
        cost_estimate=pl.CostEstimate(
            flops=2 * NODES * 2 * K * K * 3, bytes_accessed=4 * 2**20, transcendentals=0
        ),
        name="project",
    )(basis, krylov, next_map)


def shards(basis_start, admit, pattern, ground, capacity, ports, drive, corner_table, level_table):
    devices = lax.axis_size("gx") * lax.axis_size("gy")
    basis = basis_start.reshape(NODES, K)
    krylov, sums = stats(
        basis, admit, pattern, ground, capacity, ports, drive, corner_table, level_table
    )
    next_map, own = solve(
        NODES * devices, ports.shape[0] * devices, sums
    )
    swap = [(i, i ^ 1) for i in range(lax.axis_size("gx"))]
    other = lax.ppermute(own, "gx", swap)
    second = project(basis, krylov, next_map)
    even = lax.rem(lax.axis_index("gx"), 2) == 0
    response = jnp.stack([jnp.where(even, own, other), jnp.where(even, other, own)])
    return second.reshape(TX, TY, K), response


def solution(mesh):
    return jax.shard_map(
        shards,
        mesh=mesh,
        in_specs=(
            P("gx", "gy", None),
            P("gx", "gy"),
            P("gx", "gy"),
            P("gx", "gy"),
            P("gx", "gy"),
            P(("gx", "gy")),
            P(("gx", "gy"), None),
            P("gy", None),
            P(),
        ),
        out_specs=(P("gx", "gy", None), P("gy", None, None)),
        check_vma=False,
    )
```

```python
import functools
import math

import jax
import jax.numpy as jnp
from jax import lax
from jax.experimental import pallas as pl
from jax.experimental.pallas import tpu as pltpu
from jax.sharding import PartitionSpec as P

MESH = pl.DeviceIdType.MESH
highest = lax.Precision.HIGHEST
time_step = 0.25
K = 256
TX = 8
TY = 128
NODES = TX * TY
STEPS = 64
BLOCK = 128


def dot(a, b, ca=1, cb=0, precision=highest):
    return lax.dot_general(
        a, b, (((ca,), (cb,)), ((), ())), precision=precision, preferred_element_type=jnp.float32
    )


def place():
    gx, gy = lax.axis_index("gx"), lax.axis_index("gy")
    z = (gx // 4) * 2 + (gy % 4) // 2
    return gx, gy, gx % 4, gy // 4, z, gy % 2


def device(x, y, z, core):
    return ((z // 2) * 4 + x, y * 4 + (z % 2) * 2 + core)


WAVES = 5
WAVE = 512
HALF = 256
PIECE = 16
SCALES = 3 * WAVE + 264


def stats_kernel(
    basis_in, admit_in, pattern_in, ground_in, capacity_in, ports_in, drive_in,
    corners_in, levels_in, y_copy, next_map, response, out,
    basis, admit, pattern, ground, capacity, ports, drive, corners, levels, load_sem,
    y_out, y_sem,
    strength, sx, left_send, right_send, tiles, halo_row, halo_col,
    top_send, edge_send, next_row, next_col,
    v, got_core, got_plane, got_z, send_sem, recv_sem, mats, low_t, cap_mat, forcing, work,
    *, nodes, drivers,
):
    gx, gy, x, y, z, core = place()
    up = (lax.rem(gx + 15, 16), gy)
    down = (lax.rem(gx + 1, 16), gy)
    left = (gx, lax.rem(gy + 15, 16))
    right = (gx, lax.rem(gy + 1, 16))
    sibling = device(x, y, z, 1 - core)
    plane = []
    for d in sorted(range(1, 16), key=lambda d: -min(d % 4, 4 - d % 4) - min(d // 4, 4 - d // 4)):
        px, py = lax.rem(x + d % 4, 4), lax.rem(y + d // 4, 4)
        plane.append((px * 4 + py, device(px, py, z, core)))
    along_z = [device(x, y, lax.rem(z + d, 8), core) for d in (4, 3, 5, 2, 6, 1, 7)]
    barrier = pltpu.get_barrier_semaphore()
    partners = [up, down, left, right, sibling] + [p[1] for p in plane] + along_z
    for partner in partners:
        pl.semaphore_signal(barrier, inc=1, device_id=partner, device_id_type=MESH)
    loads = [
        pltpu.make_async_copy(src, dst, load_sem.at[i])
        for i, (src, dst) in enumerate(
            (
                (basis_in, basis), (admit_in, admit), (pattern_in, pattern), (ground_in, ground),
                (capacity_in, capacity), (ports_in, ports), (drive_in, drive),
                (corners_in, corners), (levels_in, levels),
            )
        )
    ]
    for copy in loads:
        copy.start()

    started = []

    def send(src, dst, target):
        i = len(started)
        copy = pltpu.make_async_remote_copy(
            src_ref=src, dst_ref=dst, send_sem=send_sem.at[i], recv_sem=recv_sem.at[i],
            device_id=target, device_id_type=MESH,
        )
        copy.start()
        started.append(copy)
        return copy

    home = x * 4 + y
    flights = {}

    def span(ref, start, size):
        return ref.at[pl.ds(pl.multiple_of(start, 8), size), :]

    def start_core(w):
        start = w * WAVE + (1 - core) * HALF
        flights[w] = [send(span(v, start, HALF), got_core.at[w], sibling)]

    def landed(w):
        for copy in flights[w]:
            copy.wait_recv()

    def start_plane(w):
        landed(w)
        start = w * WAVE + core * HALF
        rows = pl.ds(pl.multiple_of(start, 8), HALF)
        v[rows, :] = v[rows, :] + got_core[w]
        flights[w] = [
            send(span(v, start + spot * PIECE, PIECE), got_plane.at[w, i], target)
            for i, (spot, target) in enumerate(plane)
        ]

    def start_z(w):
        landed(w)
        start = w * WAVE + core * HALF + home * PIECE
        total = v[pl.ds(pl.multiple_of(start, 8), PIECE), :]
        for i in range(15):
            total = total + got_plane[w, i]
        got_z[w, z] = total
        flights[w] = [send(got_z.at[w, z], got_z.at[w, z], target) for target in along_z]

    def start_back(w):
        landed(w)
        total = got_z[w, 0]
        for i in range(1, 8):
            total = total + got_z[w, i]
        start = w * WAVE + core * HALF + home * PIECE
        out[pl.ds(pl.multiple_of(start, 8), PIECE), :] = total
        flights[w] = [
            send(span(out, start, PIECE), span(out, start, PIECE), target) for _, target in plane
        ]

    def start_last(w):
        landed(w)
        start = w * WAVE + core * HALF
        flights[w] = [send(span(out, start, HALF), span(out, start, HALF), sibling)]

    def put(w, value):
        v[pl.ds(w * WAVE, 256), :] = value[:, :128]
        v[pl.ds(w * WAVE + 256, 256), :] = value[:, 128:]

    row_id = lax.broadcasted_iota(jnp.int32, (K, K), 0)
    col_id = lax.broadcasted_iota(jnp.int32, (K, K), 1)

    def put_pair(w, lower, upper):
        put(w, jnp.where(row_id >= col_id, lower, upper))

    def gram(left_parts, right_parts):
        return sum_dot(left_parts, right_parts, 1, 0, 4)

    for copy in loads:
        copy.wait()
    strength[...] = admit[...] * pattern[...].astype(jnp.float32)
    own = strength[...]
    own_t = own.T
    cap_t = capacity[...].T
    for r in range(TX):
        rows = pl.ds(r * TY, TY)
        weighted = own_t[:, r : r + 1] * basis[rows, :]
        sx[rows, :] = weighted
        left_send[r : r + 1, :] = weighted[0:1, :]
        right_send[r : r + 1, :] = weighted[TY - 1 : TY, :]

    def capped(ref):
        return jnp.concatenate(
            [cap_t[:, r : r + 1] * ref[pl.ds(r * TY, TY), :] for r in range(TX)], 0
        )

    x_parts = split(basis[...], 2)
    xt_parts = split(basis[...].T, 2)
    cap_x = capped(basis)
    put_pair(0, gram(xt_parts, x_parts), gram(xt_parts, split(cap_x, 2)))

    pl.semaphore_wait(barrier, len(partners))
    last = (TX - 1) * TY
    halo = [
        send(strength, tiles.at[0], down),
        send(strength, tiles.at[1], up),
        send(strength, tiles.at[2], right),
        send(strength, tiles.at[3], left),
        send(sx.at[pl.ds(last, TY), :], halo_row.at[0], down),
        send(sx.at[pl.ds(0, TY), :], halo_row.at[1], up),
        send(right_send, halo_col.at[0], right),
        send(left_send, halo_col.at[1], left),
    ]
    start_core(0)
    node = lax.broadcasted_iota(jnp.int32, (8, NODES), 1)
    driver = lax.broadcasted_iota(jnp.int32, (8, NODES), 0)
    spot = jnp.full((8, NODES), -1, jnp.int32)
    for d in range(8):
        spot = jnp.where(driver == d, ports[d], spot)
    picked = (node == spot).astype(jnp.float32)
    v[pl.ds(3 * WAVE, 256), 0:STEPS] = dot(dot(picked, basis[...]), drive[...], 0, 0)
    start_plane(0)

    for copy in halo:
        copy.wait_recv()
    has_up, has_down = gx > 0, gx < 15
    has_left, has_right = gy > 0, gy < 15
    above = jnp.where(has_up, tiles[0, TX - 1 : TX, :], 0.0)
    below = jnp.where(has_down, tiles[1, 0:1, :], 0.0)
    before = jnp.where(has_left, tiles[2, :, TY - 1 : TY], 0.0)
    after = jnp.where(has_right, tiles[3, :, 0:1], 0.0)
    degree = (
        jnp.concatenate([above, own[:-1]], 0)
        + jnp.concatenate([own[1:], below], 0)
        + jnp.concatenate([before, own[:, :-1]], 1)
        + jnp.concatenate([own[:, 1:], after], 1)
    )
    diagonal_t = (ground[...] + own * degree).T
    place_in_row = lax.broadcasted_iota(jnp.int32, (TY, K), 0)

    def moved_back(block, edge):
        return jnp.where(place_in_row == TY - 1, edge, pltpu.roll(block, TY - 1, 0))

    def moved_on(block, edge):
        return jnp.where(place_in_row == 0, edge, pltpu.roll(block, 1, 0))

    halo_up = jnp.where(has_up, halo_row[0], 0.0)
    halo_down = jnp.where(has_down, halo_row[1], 0.0)
    halo_left = jnp.where(has_left, halo_col[0], 0.0)
    halo_right = jnp.where(has_right, halo_col[1], 0.0)
    inverse_t = 1.0 / cap_t
    for r in range(TX):
        rows = pl.ds(r * TY, TY)
        here = sx[rows, :]
        total = moved_on(here, halo_left[r : r + 1]) + moved_back(here, halo_right[r : r + 1])
        total = total + (halo_up if r == 0 else sx[pl.ds((r - 1) * TY, TY), :])
        total = total + (halo_down if r == TX - 1 else sx[pl.ds((r + 1) * TY, TY), :])
        image = diagonal_t[:, r : r + 1] * basis[rows, :] - own_t[:, r : r + 1] * total
        krylov = image * inverse_t[:, r : r + 1]
        y_out[rows, :] = krylov
        weighted = own_t[:, r : r + 1] * krylov
        if r == 0:
            top_send[...] = weighted
        edge_send[r : r + 1, :] = weighted[0:1, :]
    y_store = pltpu.make_async_copy(y_out, y_copy, y_sem)
    y_store.start()
    border = [send(top_send, next_row, up), send(edge_send, next_col, left)]

    y_parts = split(y_out[...], 2)
    put(1, gram(xt_parts, y_parts))
    start_core(1)
    cap_y = capped(y_out)
    v[pl.ds(3 * WAVE, 256), STEPS:128] = dot(dot(picked, y_out[...]), drive[...], 0, 0)
    v[pl.ds(3 * WAVE + 256, 256), :] = jnp.zeros((256, 128), jnp.float32)
    for i, squares in enumerate(
        (basis[...] * cap_x, basis[...] * cap_y, y_out[...] * cap_y)
    ):
        along = jnp.sum(squares, axis=0, keepdims=True)
        v[3 * WAVE + 256 + 2 * i : 3 * WAVE + 257 + 2 * i, :] = along[:, :128]
        v[3 * WAVE + 257 + 2 * i : 3 * WAVE + 258 + 2 * i, :] = along[:, 128:]
    start_core(3)
    start_plane(1)
    yt_parts = split(y_out[...].T, 2)
    cap_parts = split(cap_y, 2)
    cross = gram(xt_parts, cap_parts)
    put_pair(2, gram(yt_parts, y_parts), 0.5 * (cross + cross.T))
    start_core(2)
    start_plane(3)
    start_z(0)
    tail = gram(yt_parts, cap_parts)
    start_plane(2)

    for copy in border:
        copy.wait_recv()
    for copy in halo:
        copy.wait_send()
    bottom = jnp.where(has_down, next_row[...], 0.0)
    side = jnp.where(has_right, next_col[...], 0.0)
    for r in range(TX):
        rows = pl.ds(r * TY, TY)
        sx[rows, :] = own_t[:, r : r + 1] * y_out[rows, :]
    for r in range(TX):
        rows = pl.ds(r * TY, TY)
        total = moved_back(sx[rows, :], side[r : r + 1])
        total = total + (bottom if r == TX - 1 else sx[pl.ds((r + 1) * TY, TY), :])
        sx[rows, :] = (
            0.5 * diagonal_t[:, r : r + 1] * y_out[rows, :] - own_t[:, r : r + 1] * total
        )
    start_z(1)
    half = gram(yt_parts, split(sx[...], 2))
    put_pair(4, half + half.T, tail)
    start_core(4)
    start_back(0)
    start_z(3)
    start_plane(4)
    start_z(2)
    start_back(1)
    start_last(0)
    start_back(3)
    start_back(2)
    start_z(4)
    for w in (1, 3, 2):
        start_last(w)
    start_back(4)
    start_last(4)
    for w in range(WAVES):
        landed(w)
    y_store.wait()
    for copy in started[len(halo) :]:
        copy.wait_send()
    for kind in range(3):
        for k in range(2):
            level = levels[kind, 0]
            for i in range(1, 4):
                level = jnp.where(corners[k, kind] == i, levels[kind, i], level)
            out[SCALES + 2 * kind + k : SCALES + 2 * kind + k + 1, :] = jnp.full((1, 128), level, jnp.float32)
    solve_sums(
        nodes, drivers, out, next_map, response, mats, low_t, cap_mat, forcing, work
    )


def stats(nodes, drivers, basis, admit, pattern, ground, capacity, ports, drive, corners, levels):
    vmem = pl.BlockSpec(memory_space=pltpu.VMEM)
    anywhere = pl.BlockSpec(memory_space=pl.ANY)
    f32 = jnp.float32
    copies = 8 + 2 + WAVES * (1 + 15 + 7 + 15 + 1)
    return pl.pallas_call(
        functools.partial(stats_kernel, nodes=nodes, drivers=drivers),
        out_shape=(
            jax.ShapeDtypeStruct((NODES, K), f32),
            jax.ShapeDtypeStruct((K, 2 * K), f32),
            jax.ShapeDtypeStruct((STEPS, 2 * K), f32),
        ),
        in_specs=[anywhere] * 9,
        out_specs=(anywhere, vmem, vmem),
        scratch_shapes=[
            pltpu.VMEM((WAVES * WAVE, 128), f32),
            pltpu.VMEM((NODES, K), f32),
            pltpu.VMEM((TX, TY), f32),
            pltpu.VMEM((TX, TY), jnp.int32),
            pltpu.VMEM((TX, TY), f32),
            pltpu.VMEM((TX, TY), f32),
            pltpu.SMEM((8,), jnp.int32),
            pltpu.VMEM((8, STEPS), f32),
            pltpu.SMEM((2, 3), jnp.int32),
            pltpu.SMEM((3, 4), f32),
            pltpu.SemaphoreType.DMA((9,)),
            pltpu.VMEM((NODES, K), f32),
            pltpu.SemaphoreType.DMA,
            pltpu.VMEM((TX, TY), f32),
            pltpu.VMEM((NODES, K), f32),
            pltpu.VMEM((TX, K), f32),
            pltpu.VMEM((TX, K), f32),
            pltpu.VMEM((4, TX, TY), f32),
            pltpu.VMEM((2, TY, K), f32),
            pltpu.VMEM((2, TX, K), f32),
            pltpu.VMEM((TY, K), f32),
            pltpu.VMEM((TX, K), f32),
            pltpu.VMEM((TY, K), f32),
            pltpu.VMEM((TX, K), f32),
            pltpu.VMEM((WAVES * WAVE, 128), f32),
            pltpu.VMEM((WAVES, HALF, 128), f32),
            pltpu.VMEM((WAVES, 15, PIECE, 128), f32),
            pltpu.VMEM((WAVES, 8, PIECE, 128), f32),
            pltpu.SemaphoreType.DMA((copies,)),
            pltpu.SemaphoreType.DMA((copies,)),
            pltpu.VMEM((2, 512, 512), f32),
            pltpu.VMEM((512, 512), f32),
            pltpu.VMEM((512, 512), f32),
            pltpu.VMEM((512, STEPS), f32),
            pltpu.VMEM((2, BLOCK, 2 * BLOCK), f32),
        ],
        compiler_params=pltpu.CompilerParams(
            collective_id=0, has_side_effects=True, vmem_limit_bytes=65024 * 1024
        ),
        name="stats",
    )(basis, admit, pattern, ground, capacity, ports, drive, corners, levels)


def split(a, count):
    parts = []
    for _ in range(count - 1):
        part = a.astype(jnp.bfloat16)
        parts.append(part)
        a = a - part.astype(jnp.float32)
    return parts + [a.astype(jnp.bfloat16)]


PAIRS = {
    2: ((0, 0), (0, 1), (1, 0)),
    4: ((0, 0), (0, 1), (1, 0), (1, 1)),
    3: ((0, 0), (0, 1), (1, 0), (1, 1), (0, 2), (2, 0)),
}


def deep_dot(a, b, ca, cb, count=3):
    pairs = PAIRS[count]
    left = jnp.concatenate([a[i] for i, j in pairs], ca)
    right = jnp.concatenate([b[j] for i, j in pairs], cb)
    return lax.dot_general(
        left, right, (((ca,), (cb,)), ((), ())), preferred_element_type=jnp.float32
    )


def sum_dot(a, b, ca=1, cb=0, count=2):
    total = None
    for i, j in PAIRS[count]:
        term = lax.dot_general(
            a[i], b[j], (((ca,), (cb,)), ((), ())), preferred_element_type=jnp.float32
        )
        total = term if total is None else total + term
    return total


def solve_sums(
    nodes, drivers, sums, next_map, response,
    mats, low_t, cap_mat, forcing, work,
):
    scale = 1.0 / nodes

    row_id = lax.broadcasted_iota(jnp.int32, (K, K), 0)
    col_id = lax.broadcasted_iota(jnp.int32, (K, K), 1)

    def take(w):
        start = w * WAVE
        return (
            jnp.concatenate([sums[pl.ds(start, 256), :], sums[pl.ds(start + 256, 256), :]], 1)
            * scale
        )

    def take_pair(w, place):
        both = take(w)
        turned = both.T
        at = 3 * WAVE + 256 + 2 * place
        diag = jnp.concatenate([sums[at : at + 1, :], sums[at + 1 : at + 2, :]], 1) * scale
        lower = jnp.where(row_id >= col_id, both, turned)
        upper = jnp.where(row_id < col_id, both, jnp.where(row_id == col_id, diag, turned))
        return lower, upper

    xx, xcx = take_pair(0, 0)
    xy = take(1)
    yy, xcy = take_pair(2, 1)
    cond_tail, ycy = take_pair(4, 2)
    mats[0, :256, :256] = xx
    mats[0, :256, 256:] = xy
    mats[0, 256:, 256:] = yy
    cap_mat[:256, :256] = xcx
    cap_mat[:256, 256:] = xcy
    cap_mat[256:, :256] = xcy
    cap_mat[256:, 256:] = ycy
    k = lax.rem(lax.axis_index("gx"), 2)
    g, ratio, gain = [
        jnp.where(
            k == 0,
            sums[SCALES + 2 * i : SCALES + 2 * i + 1, 0:1],
            sums[SCALES + 2 * i + 1 : SCALES + 2 * i + 2, 0:1],
        )
        for i in range(3)
    ]
    ratio = ratio * (1.0 / time_step)
    mats[1, :256, :256] = g * xcy + ratio * xcx
    mats[1, :256, 256:] = g * ycy + ratio * xcy
    mats[1, 256:, 256:] = g * cond_tail + ratio * ycy
    part = sums[pl.ds(3 * WAVE, 256), :] * (1.0 / math.sqrt(drivers))
    forcing[:256, :] = part[:, :STEPS]
    forcing[256:, :] = part[:, STEPS:]
    for m in range(2):
        mats[m, 256:, :256] = jnp.zeros((256, 256), jnp.float32)

    sub = lax.broadcasted_iota(jnp.int32, (8, 128), 0)
    row_id = lax.broadcasted_iota(jnp.int32, (BLOCK, BLOCK), 0)
    col_id = lax.broadcasted_iota(jnp.int32, (BLOCK, BLOCK), 1)
    eye = (row_id == col_id).astype(jnp.float32)

    def eliminate(rows, lo, first):
        tiles = range(first, 4)
        at = lo + 8 * first
        cols = {
            t: [jnp.broadcast_to(rows[t][0][:, at + k : at + k + 1], (8, 128)) for k in range(8)]
            for t in tiles
        }
        pivots = None
        for i in range(8):
            pivot = jnp.broadcast_to(cols[first][i][i : i + 1, :], (8, 128))
            inverse = 1.0 / pivot
            pivots = pivot if pivots is None else jnp.where(sub == i, pivot, pivots)
            below = {t: cols[t][i] * inverse for t in tiles}
            below[first] = jnp.where(sub > i, below[first], 0.0)
            for k in range(i + 1, 8):
                top = jnp.broadcast_to(cols[first][k][i : i + 1, :], (8, 128))
                for t in tiles:
                    cols[t][k] = cols[t][k] - below[t] * top
            for h in range(2):
                top = jnp.broadcast_to(rows[first][h][i : i + 1, :], (8, 128))
                for t in tiles:
                    rows[t][h] = rows[t][h] - below[t] * top
        root = lax.rsqrt(pivots)
        return [rows[first][h] * root for h in range(2)]

    def factor_panel(lo):
        done = lo + 32
        rows = [
            [[work[m, lo + 8 * t : lo + 8 * t + 8, h * 128 : h * 128 + 128] for h in range(2)]
             for t in range(4)]
            for m in range(2)
        ]
        final = [[None] * 4, [None] * 4]
        for t in range(4):
            for m in range(2):
                final[m][t] = eliminate(rows[m], lo, t)
        for m in range(2):
            panel = jnp.concatenate([jnp.concatenate(final[m][t], 1) for t in range(4)], 0)
            work[m, lo:done, :] = panel
            if done < BLOCK:
                parts = split(panel, 3)
                update = deep_dot([p[:, :BLOCK] for p in parts], parts, 0, 0)
                work[m, done:, :] = work[m, done:, :] - update[done:, :]

    def step(s, carry):
        lo = pl.multiple_of(s * BLOCK, BLOCK)
        for m in range(2):
            work[m, :, :BLOCK] = mats[m, pl.ds(lo, BLOCK), pl.ds(lo, BLOCK)]
            work[m, :, BLOCK:] = eye
        for p in range(BLOCK // 32):
            factor_panel(32 * p)
        low_t[pl.ds(lo, BLOCK), pl.ds(lo, BLOCK)] = jnp.where(
            row_id <= col_id, work[0, :, :BLOCK], 0.0
        )
        for i in range(4):

            @pl.when(s == i)
            def _():
                lo, hi = i * BLOCK, (i + 1) * BLOCK
                for m in range(2):
                    corner = jnp.where(row_id >= col_id, work[m, :, BLOCK:], 0.0)
                    row = deep_dot(split(corner, 3), split(mats[m, lo:hi, :], 3), 1, 0)
                    if i > 0:
                        mats[m, lo:hi, :lo] = row[:, :lo]
                    mats[m, lo:hi, lo:hi] = corner
                    if i < 3:
                        mats[m, lo:hi, hi:] = jnp.zeros((BLOCK, 512 - hi), jnp.float32)
                        if m == 0:
                            low_t[lo:hi, hi:] = row[:, hi:]
                        left = [row[:, :lo]] if i > 0 else []
                        row = jnp.concatenate(left + [corner, row[:, hi:]], 1)
                        parts = split(row, 3)
                        update = deep_dot([p[:, hi:] for p in parts], parts, 0, 0)
                        if i > 0:
                            mats[m, hi:, :lo] = mats[m, hi:, :lo] - update[:, :lo]
                        mats[m, hi:, lo:hi] = -update[:, lo:hi]
                        mats[m, hi:, hi:] = mats[m, hi:, hi:] - update[:, hi:]

        return carry

    low_t[...] = jnp.zeros_like(low_t)
    lax.fori_loop(0, 4, step, 0)

    next_map[...] = mats[0, 256:, :]
    low = split(mats[1], 2)
    half_way = sum_dot(low, split(cap_mat[...] * ratio, 2))
    power = sum_dot(split(half_way, 2), low, 1, 1)
    states = sum_dot(split(forcing[...] * gain, 2), low, 0, 1)
    time = lax.broadcasted_iota(jnp.int32, (STEPS, 512), 0)
    s = 1
    while s < STEPS:
        late = jnp.where(time >= s, pltpu.roll(states, s, 0), 0.0)
        parts = split(power, 2)
        late_parts = split(late, 2)
        if 2 * s < STEPS:
            both = sum_dot(
                [jnp.concatenate([p, q], 0) for p, q in zip(parts, late_parts)], parts
            )
            power = both[:512]
            states = states + both[512:]
        else:
            states = states + sum_dot(late_parts, parts)
        s *= 2
    states = sum_dot(split(states, 2), low)
    response[...] = sum_dot(split(states, 2), split(low_t[...], 2), 1, 1)


def project_kernel(basis_in, krylov_in, next_map_in, second, basis, krylov, next_map, load_sem):
    loads = [
        pltpu.make_async_copy(src, dst, load_sem.at[i])
        for i, (src, dst) in enumerate(
            ((next_map_in, next_map), (basis_in, basis), (krylov_in, krylov))
        )
    ]
    for copy in loads:
        copy.start()
    loads[0].wait()
    maps = split(next_map[...], 2)
    loads[1].wait()
    loads[2].wait()
    for c in range(4):
        rows = pl.ds(c * 256, 256)
        second[rows, :] = sum_dot(
            split(basis[rows, :], 2), [m[:, :256] for m in maps], 1, 1
        ) + sum_dot(split(krylov[rows, :], 2), [m[:, 256:] for m in maps], 1, 1)


def project(basis, krylov, next_map):
    anywhere = pl.BlockSpec(memory_space=pltpu.HBM)
    f32 = jnp.float32
    return pl.pallas_call(
        project_kernel,
        out_shape=jax.ShapeDtypeStruct((NODES, K), f32),
        in_specs=[anywhere] * 3,
        out_specs=pl.BlockSpec(memory_space=pltpu.VMEM),
        scratch_shapes=[
            pltpu.VMEM((NODES, K), f32),
            pltpu.VMEM((NODES, K), f32),
            pltpu.VMEM((K, 2 * K), f32),
            pltpu.SemaphoreType.DMA((3,)),
        ],
        compiler_params=pltpu.CompilerParams(vmem_limit_bytes=65024 * 1024),
        cost_estimate=pl.CostEstimate(
            flops=2 * NODES * 2 * K * K * 3, bytes_accessed=4 * 2**20, transcendentals=0
        ),
        name="project",
    )(basis, krylov, next_map)


def shards(basis_start, admit, pattern, ground, capacity, ports, drive, corner_table, level_table):
    devices = lax.axis_size("gx") * lax.axis_size("gy")
    basis = basis_start.reshape(NODES, K)
    krylov, next_map, own = stats(
        NODES * devices, ports.shape[0] * devices,
        basis, admit, pattern, ground, capacity, ports, drive, corner_table, level_table,
    )
    swap = [(i, i ^ 1) for i in range(lax.axis_size("gx"))]
    other = lax.ppermute(own, "gx", swap)
    second = project(basis, krylov, next_map)
    even = lax.rem(lax.axis_index("gx"), 2) == 0
    response = jnp.stack([jnp.where(even, own, other), jnp.where(even, other, own)])
    return second.reshape(TX, TY, K), response


def solution(mesh):
    return jax.shard_map(
        shards,
        mesh=mesh,
        in_specs=(
            P("gx", "gy", None),
            P("gx", "gy"),
            P("gx", "gy"),
            P("gx", "gy"),
            P("gx", "gy"),
            P(("gx", "gy")),
            P(("gx", "gy"), None),
            P("gy", None),
            P(),
        ),
        out_specs=(P("gx", "gy", None), P("gy", None, None)),
        check_vma=False,
    )
```

```python
import functools
import math

import jax
import jax.numpy as jnp
from jax import lax
from jax.experimental import pallas as pl
from jax.experimental.pallas import tpu as pltpu
from jax.sharding import PartitionSpec as P

MESH = pl.DeviceIdType.MESH
highest = lax.Precision.HIGHEST
time_step = 0.25
K = 256
TX = 8
TY = 128
NODES = TX * TY
STEPS = 64
BLOCK = 128


def dot(a, b, ca=1, cb=0, precision=highest):
    return lax.dot_general(
        a, b, (((ca,), (cb,)), ((), ())), precision=precision, preferred_element_type=jnp.float32
    )


def place():
    gx, gy = lax.axis_index("gx"), lax.axis_index("gy")
    z = (gx // 4) * 2 + (gy % 4) // 2
    return gx, gy, gx % 4, gy // 4, z, gy % 2


def device(x, y, z, core):
    return ((z // 2) * 4 + x, y * 4 + (z % 2) * 2 + core)


WAVES = 5
WAVE = 512
HALF = 256
PIECE = 16


def stats_kernel(
    basis_in, admit_in, pattern_in, ground_in, capacity_in, ports_in, drive_in,
    corners_in, levels_in, y_copy, next_map, response, out,
    basis, admit, pattern, ground, capacity, ports, drive, corners, levels, load_sem,
    y_out, y_sem,
    strength, sx, left_send, right_send, tiles, halo_row, halo_col,
    top_send, edge_send, next_row, next_col,
    v, got_core, got_plane, got_z, send_sem, recv_sem, mats, low_t, cap_mat, forcing, work,
    *, nodes, drivers,
):
    gx, gy, x, y, z, core = place()
    up = (lax.rem(gx + 15, 16), gy)
    down = (lax.rem(gx + 1, 16), gy)
    left = (gx, lax.rem(gy + 15, 16))
    right = (gx, lax.rem(gy + 1, 16))
    sibling = device(x, y, z, 1 - core)
    plane = []
    for d in sorted(range(1, 16), key=lambda d: -min(d % 4, 4 - d % 4) - min(d // 4, 4 - d // 4)):
        px, py = lax.rem(x + d % 4, 4), lax.rem(y + d // 4, 4)
        plane.append((px * 4 + py, device(px, py, z, core)))
    along_z = [device(x, y, lax.rem(z + d, 8), core) for d in (4, 3, 5, 2, 6, 1, 7)]
    barrier = pltpu.get_barrier_semaphore()
    partners = [up, down, left, right, sibling] + [p[1] for p in plane] + along_z
    for partner in partners:
        pl.semaphore_signal(barrier, inc=1, device_id=partner, device_id_type=MESH)
    loads = [
        pltpu.make_async_copy(src, dst, load_sem.at[i])
        for i, (src, dst) in enumerate(
            (
                (basis_in, basis), (admit_in, admit), (pattern_in, pattern), (ground_in, ground),
                (capacity_in, capacity), (ports_in, ports), (drive_in, drive),
                (corners_in, corners), (levels_in, levels),
            )
        )
    ]
    for copy in loads:
        copy.start()

    started = []

    def send(src, dst, target):
        i = len(started)
        copy = pltpu.make_async_remote_copy(
            src_ref=src, dst_ref=dst, send_sem=send_sem.at[i], recv_sem=recv_sem.at[i],
            device_id=target, device_id_type=MESH,
        )
        copy.start()
        started.append(copy)
        return copy

    home = x * 4 + y
    flights = {}

    def span(ref, start, size):
        return ref.at[pl.ds(pl.multiple_of(start, 8), size), :]

    def start_core(w):
        start = w * WAVE + (1 - core) * HALF
        flights[w] = [send(span(v, start, HALF), got_core.at[w], sibling)]

    def landed(w):
        for copy in flights[w]:
            copy.wait_recv()

    def start_plane(w):
        landed(w)
        start = w * WAVE + core * HALF
        rows = pl.ds(pl.multiple_of(start, 8), HALF)
        v[rows, :] = v[rows, :] + got_core[w]
        flights[w] = [
            send(span(v, start + spot * PIECE, PIECE), got_plane.at[w, i], target)
            for i, (spot, target) in enumerate(plane)
        ]

    def start_z(w):
        landed(w)
        start = w * WAVE + core * HALF + home * PIECE
        total = v[pl.ds(pl.multiple_of(start, 8), PIECE), :]
        for i in range(15):
            total = total + got_plane[w, i]
        got_z[w, z] = total
        flights[w] = [send(got_z.at[w, z], got_z.at[w, z], target) for target in along_z]

    def start_back(w):
        landed(w)
        total = got_z[w, 0]
        for i in range(1, 8):
            total = total + got_z[w, i]
        start = w * WAVE + core * HALF + home * PIECE
        out[pl.ds(pl.multiple_of(start, 8), PIECE), :] = total
        flights[w] = [
            send(span(out, start, PIECE), span(out, start, PIECE), target) for _, target in plane
        ]

    def start_last(w):
        landed(w)
        start = w * WAVE + core * HALF
        flights[w] = [send(span(out, start, HALF), span(out, start, HALF), sibling)]

    def put(w, value):
        v[pl.ds(w * WAVE, 256), :] = value[:, :128]
        v[pl.ds(w * WAVE + 256, 256), :] = value[:, 128:]

    row_id = lax.broadcasted_iota(jnp.int32, (K, K), 0)
    col_id = lax.broadcasted_iota(jnp.int32, (K, K), 1)

    def put_pair(w, lower, upper):
        put(w, jnp.where(row_id >= col_id, lower, upper))

    def gram(left_parts, right_parts):
        return sum_dot(left_parts, right_parts, 1, 0, 4)

    for copy in loads:
        copy.wait()
    strength[...] = admit[...] * pattern[...].astype(jnp.float32)
    own = strength[...]
    own_t = own.T
    cap_t = capacity[...].T
    for r in range(TX):
        rows = pl.ds(r * TY, TY)
        weighted = own_t[:, r : r + 1] * basis[rows, :]
        sx[rows, :] = weighted
        left_send[r : r + 1, :] = weighted[0:1, :]
        right_send[r : r + 1, :] = weighted[TY - 1 : TY, :]

    def capped(ref):
        return jnp.concatenate(
            [cap_t[:, r : r + 1] * ref[pl.ds(r * TY, TY), :] for r in range(TX)], 0
        )

    x_parts = split(basis[...], 2)
    xt_parts = split(basis[...].T, 2)
    cap_x = capped(basis)
    put_pair(0, gram(xt_parts, x_parts), gram(xt_parts, split(cap_x, 2)))

    pl.semaphore_wait(barrier, len(partners))
    last = (TX - 1) * TY
    halo = [
        send(strength, tiles.at[0], down),
        send(strength, tiles.at[1], up),
        send(strength, tiles.at[2], right),
        send(strength, tiles.at[3], left),
        send(sx.at[pl.ds(last, TY), :], halo_row.at[0], down),
        send(sx.at[pl.ds(0, TY), :], halo_row.at[1], up),
        send(right_send, halo_col.at[0], right),
        send(left_send, halo_col.at[1], left),
    ]
    start_core(0)
    node = lax.broadcasted_iota(jnp.int32, (8, NODES), 1)
    driver = lax.broadcasted_iota(jnp.int32, (8, NODES), 0)
    spot = jnp.full((8, NODES), -1, jnp.int32)
    for d in range(8):
        spot = jnp.where(driver == d, ports[d], spot)
    picked = (node == spot).astype(jnp.float32)
    v[pl.ds(3 * WAVE, 256), 0:STEPS] = dot(dot(picked, basis[...]), drive[...], 0, 0)
    start_plane(0)

    for copy in halo:
        copy.wait_recv()
    has_up, has_down = gx > 0, gx < 15
    has_left, has_right = gy > 0, gy < 15
    above = jnp.where(has_up, tiles[0, TX - 1 : TX, :], 0.0)
    below = jnp.where(has_down, tiles[1, 0:1, :], 0.0)
    before = jnp.where(has_left, tiles[2, :, TY - 1 : TY], 0.0)
    after = jnp.where(has_right, tiles[3, :, 0:1], 0.0)
    degree = (
        jnp.concatenate([above, own[:-1]], 0)
        + jnp.concatenate([own[1:], below], 0)
        + jnp.concatenate([before, own[:, :-1]], 1)
        + jnp.concatenate([own[:, 1:], after], 1)
    )
    diagonal_t = (ground[...] + own * degree).T
    place_in_row = lax.broadcasted_iota(jnp.int32, (TY, K), 0)

    def moved_back(block, edge):
        return jnp.where(place_in_row == TY - 1, edge, pltpu.roll(block, TY - 1, 0))

    def moved_on(block, edge):
        return jnp.where(place_in_row == 0, edge, pltpu.roll(block, 1, 0))

    halo_up = jnp.where(has_up, halo_row[0], 0.0)
    halo_down = jnp.where(has_down, halo_row[1], 0.0)
    halo_left = jnp.where(has_left, halo_col[0], 0.0)
    halo_right = jnp.where(has_right, halo_col[1], 0.0)
    inverse_t = 1.0 / cap_t
    for r in range(TX):
        rows = pl.ds(r * TY, TY)
        here = sx[rows, :]
        total = moved_on(here, halo_left[r : r + 1]) + moved_back(here, halo_right[r : r + 1])
        total = total + (halo_up if r == 0 else sx[pl.ds((r - 1) * TY, TY), :])
        total = total + (halo_down if r == TX - 1 else sx[pl.ds((r + 1) * TY, TY), :])
        image = diagonal_t[:, r : r + 1] * basis[rows, :] - own_t[:, r : r + 1] * total
        krylov = image * inverse_t[:, r : r + 1]
        y_out[rows, :] = krylov
        weighted = own_t[:, r : r + 1] * krylov
        if r == 0:
            top_send[...] = weighted
        edge_send[r : r + 1, :] = weighted[0:1, :]
    y_store = pltpu.make_async_copy(y_out, y_copy, y_sem)
    y_store.start()
    border = [send(top_send, next_row, up), send(edge_send, next_col, left)]

    y_parts = split(y_out[...], 2)
    put(1, gram(xt_parts, y_parts))
    start_core(1)
    cap_y = capped(y_out)
    v[pl.ds(3 * WAVE, 256), STEPS:128] = dot(dot(picked, y_out[...]), drive[...], 0, 0)
    v[pl.ds(3 * WAVE + 256, 256), :] = jnp.zeros((256, 128), jnp.float32)
    for i, squares in enumerate(
        (basis[...] * cap_x, basis[...] * cap_y, y_out[...] * cap_y)
    ):
        along = jnp.sum(squares, axis=0, keepdims=True)
        v[3 * WAVE + 256 + 2 * i : 3 * WAVE + 257 + 2 * i, :] = along[:, :128]
        v[3 * WAVE + 257 + 2 * i : 3 * WAVE + 258 + 2 * i, :] = along[:, 128:]
    start_core(3)
    start_plane(1)
    yt_parts = split(y_out[...].T, 2)
    cap_parts = split(cap_y, 2)
    cross = gram(xt_parts, cap_parts)
    put_pair(2, gram(yt_parts, y_parts), 0.5 * (cross + cross.T))
    start_core(2)
    start_plane(3)
    start_z(0)
    tail = gram(yt_parts, cap_parts)
    start_plane(2)

    for copy in border:
        copy.wait_recv()
    for copy in halo:
        copy.wait_send()
    bottom = jnp.where(has_down, next_row[...], 0.0)
    side = jnp.where(has_right, next_col[...], 0.0)
    for r in range(TX):
        rows = pl.ds(r * TY, TY)
        sx[rows, :] = own_t[:, r : r + 1] * y_out[rows, :]
    for r in range(TX):
        rows = pl.ds(r * TY, TY)
        total = moved_back(sx[rows, :], side[r : r + 1])
        total = total + (bottom if r == TX - 1 else sx[pl.ds((r + 1) * TY, TY), :])
        sx[rows, :] = (
            0.5 * diagonal_t[:, r : r + 1] * y_out[rows, :] - own_t[:, r : r + 1] * total
        )
    start_z(1)
    half = gram(yt_parts, split(sx[...], 2))
    put_pair(4, half + half.T, tail)
    start_core(4)
    start_back(0)
    start_z(3)
    start_plane(4)
    start_z(2)
    start_back(1)
    start_last(0)
    start_back(3)
    start_back(2)
    start_z(4)
    basis_first, basis_second, corner_early, corner = solver(
        nodes, drivers, out, next_map, response, mats, low_t, cap_mat, forcing, work
    )
    landed(0)
    basis_first()
    for w in (1, 3, 2):
        start_last(w)
    start_back(4)
    for w in (1, 3, 2):
        landed(w)
    basis_second()
    start_last(4)
    corner_early()
    y_store.wait()
    for copy in started[len(halo) :]:
        copy.wait_send()
    landed(4)
    odd = lax.rem(gx, 2)
    scales = []
    for kind in range(3):
        pair = []
        for k in range(2):
            level = levels[kind, 0]
            for i in range(1, 4):
                level = jnp.where(corners[k, kind] == i, levels[kind, i], level)
            pair.append(level)
        scales.append(jnp.where(odd == 0, pair[0], pair[1]))
    corner(*scales)


def stats(nodes, drivers, basis, admit, pattern, ground, capacity, ports, drive, corners, levels):
    vmem = pl.BlockSpec(memory_space=pltpu.VMEM)
    anywhere = pl.BlockSpec(memory_space=pl.ANY)
    f32 = jnp.float32
    copies = 8 + 2 + WAVES * (1 + 15 + 7 + 15 + 1)
    return pl.pallas_call(
        functools.partial(stats_kernel, nodes=nodes, drivers=drivers),
        out_shape=(
            jax.ShapeDtypeStruct((NODES, K), f32),
            jax.ShapeDtypeStruct((K, 2 * K), f32),
            jax.ShapeDtypeStruct((STEPS, 2 * K), f32),
        ),
        in_specs=[anywhere] * 9,
        out_specs=(anywhere, vmem, vmem),
        scratch_shapes=[
            pltpu.VMEM((WAVES * WAVE, 128), f32),
            pltpu.VMEM((NODES, K), f32),
            pltpu.VMEM((TX, TY), f32),
            pltpu.VMEM((TX, TY), jnp.int32),
            pltpu.VMEM((TX, TY), f32),
            pltpu.VMEM((TX, TY), f32),
            pltpu.SMEM((8,), jnp.int32),
            pltpu.VMEM((8, STEPS), f32),
            pltpu.SMEM((2, 3), jnp.int32),
            pltpu.SMEM((3, 4), f32),
            pltpu.SemaphoreType.DMA((9,)),
            pltpu.VMEM((NODES, K), f32),
            pltpu.SemaphoreType.DMA,
            pltpu.VMEM((TX, TY), f32),
            pltpu.VMEM((NODES, K), f32),
            pltpu.VMEM((TX, K), f32),
            pltpu.VMEM((TX, K), f32),
            pltpu.VMEM((4, TX, TY), f32),
            pltpu.VMEM((2, TY, K), f32),
            pltpu.VMEM((2, TX, K), f32),
            pltpu.VMEM((TY, K), f32),
            pltpu.VMEM((TX, K), f32),
            pltpu.VMEM((TY, K), f32),
            pltpu.VMEM((TX, K), f32),
            pltpu.VMEM((WAVES * WAVE, 128), f32),
            pltpu.VMEM((WAVES, HALF, 128), f32),
            pltpu.VMEM((WAVES, 15, PIECE, 128), f32),
            pltpu.VMEM((WAVES, 8, PIECE, 128), f32),
            pltpu.SemaphoreType.DMA((copies,)),
            pltpu.SemaphoreType.DMA((copies,)),
            pltpu.VMEM((2, 512, 512), f32),
            pltpu.VMEM((512, 512), f32),
            pltpu.VMEM((512, 512), f32),
            pltpu.VMEM((512, STEPS), f32),
            pltpu.VMEM((2, BLOCK, 2 * BLOCK), f32),
        ],
        compiler_params=pltpu.CompilerParams(
            collective_id=0, has_side_effects=True, vmem_limit_bytes=65024 * 1024
        ),
        name="stats",
    )(basis, admit, pattern, ground, capacity, ports, drive, corners, levels)


def split(a, count):
    parts = []
    for _ in range(count - 1):
        part = a.astype(jnp.bfloat16)
        parts.append(part)
        a = a - part.astype(jnp.float32)
    return parts + [a.astype(jnp.bfloat16)]


PAIRS = {
    2: ((0, 0), (0, 1), (1, 0)),
    4: ((0, 0), (0, 1), (1, 0), (1, 1)),
    3: ((0, 0), (0, 1), (1, 0), (1, 1), (0, 2), (2, 0)),
}


def deep_dot(a, b, ca, cb, count=3):
    pairs = PAIRS[count]
    left = jnp.concatenate([a[i] for i, j in pairs], ca)
    right = jnp.concatenate([b[j] for i, j in pairs], cb)
    return lax.dot_general(
        left, right, (((ca,), (cb,)), ((), ())), preferred_element_type=jnp.float32
    )


def sum_dot(a, b, ca=1, cb=0, count=2):
    total = None
    for i, j in PAIRS[count]:
        term = lax.dot_general(
            a[i], b[j], (((ca,), (cb,)), ((), ())), preferred_element_type=jnp.float32
        )
        total = term if total is None else total + term
    return total


def solver(nodes, drivers, sums, next_map, response, mats, low_t, cap_mat, forcing, work):
    scale = 1.0 / nodes

    wide_row = lax.broadcasted_iota(jnp.int32, (K, K), 0)
    wide_col = lax.broadcasted_iota(jnp.int32, (K, K), 1)

    def take(w):
        start = w * WAVE
        return (
            jnp.concatenate([sums[pl.ds(start, 256), :], sums[pl.ds(start + 256, 256), :]], 1)
            * scale
        )

    def take_lower(w):
        both = take(w)
        return jnp.where(wide_row >= wide_col, both, both.T)

    def take_upper(w, place):
        both = take(w)
        at = 3 * WAVE + 256 + 2 * place
        diag = jnp.concatenate([sums[at : at + 1, :], sums[at + 1 : at + 2, :]], 1) * scale
        return jnp.where(
            wide_row < wide_col, both, jnp.where(wide_row == wide_col, diag, both.T)
        )

    sub = lax.broadcasted_iota(jnp.int32, (8, 128), 0)
    row_id = lax.broadcasted_iota(jnp.int32, (BLOCK, BLOCK), 0)
    col_id = lax.broadcasted_iota(jnp.int32, (BLOCK, BLOCK), 1)

    def eliminate(rows, lo, first):
        tiles = range(first, 4)
        at = lo + 8 * first
        cols = {
            t: [jnp.broadcast_to(rows[t][0][:, at + k : at + k + 1], (8, 128)) for k in range(8)]
            for t in tiles
        }
        pivots = None
        for i in range(8):
            pivot = jnp.broadcast_to(cols[first][i][i : i + 1, :], (8, 128))
            inverse = 1.0 / pivot
            pivots = pivot if pivots is None else jnp.where(sub == i, pivot, pivots)
            below = {t: cols[t][i] * inverse for t in tiles}
            below[first] = jnp.where(sub > i, below[first], 0.0)
            for k in range(i + 1, 8):
                top = jnp.broadcast_to(cols[first][k][i : i + 1, :], (8, 128))
                for t in tiles:
                    cols[t][k] = cols[t][k] - below[t] * top
            for h in range(2):
                top = jnp.broadcast_to(rows[first][h][i : i + 1, :], (8, 128))
                for t in tiles:
                    rows[t][h] = rows[t][h] - below[t] * top
        root = lax.rsqrt(pivots)
        return [rows[first][h] * root for h in range(2)]

    def factor_panel(lo, ms):
        done = lo + 32
        rows = {
            m: [[work[m, lo + 8 * t : lo + 8 * t + 8, h * 128 : h * 128 + 128] for h in range(2)]
                for t in range(4)]
            for m in ms
        }
        final = {m: [None] * 4 for m in ms}
        for t in range(4):
            for m in ms:
                final[m][t] = eliminate(rows[m], lo, t)
        for m in ms:
            panel = jnp.concatenate([jnp.concatenate(final[m][t], 1) for t in range(4)], 0)
            work[m, lo:done, :] = panel
            if done < BLOCK:
                parts = split(panel, 3)
                update = deep_dot([p[:, :BLOCK] for p in parts], parts, 0, 0)
                work[m, done:, :] = work[m, done:, :] - update[done:, :]

    def factor_blocks(places):
        for m, place in places.items():
            lo = pl.multiple_of(place * BLOCK, BLOCK)
            work[m, :, :BLOCK] = mats[m, pl.ds(lo, BLOCK), pl.ds(lo, BLOCK)]
            work[m, :, BLOCK:] = (row_id == col_id).astype(jnp.float32)
        for p in range(BLOCK // 32):
            factor_panel(32 * p, list(places))
        if 0 in places:
            lo = pl.multiple_of(places[0] * BLOCK, BLOCK)
            low_t[pl.ds(lo, BLOCK), pl.ds(lo, BLOCK)] = jnp.where(
                row_id <= col_id, work[0, :, :BLOCK], 0.0
            )

    def finish_block(m, i):
        lo, hi = i * BLOCK, (i + 1) * BLOCK
        corner = jnp.where(row_id >= col_id, work[m, :, BLOCK:], 0.0)
        row = deep_dot(split(corner, 3), split(mats[m, lo:hi, :], 3), 1, 0)
        if i > 0:
            mats[m, lo:hi, :lo] = row[:, :lo]
        mats[m, lo:hi, lo:hi] = corner
        if i < 3:
            mats[m, lo:hi, hi:] = jnp.zeros((BLOCK, 512 - hi), jnp.float32)
            if m == 0:
                low_t[lo:hi, hi:] = row[:, hi:]
            left = [row[:, :lo]] if i > 0 else []
            row = jnp.concatenate(left + [corner, row[:, hi:]], 1)
            parts = split(row, 3)
            update = deep_dot([p[:, hi:] for p in parts], parts, 0, 0)
            if i > 0:
                mats[m, hi:, :lo] = mats[m, hi:, :lo] - update[:, :lo]
            mats[m, hi:, lo:hi] = -update[:, lo:hi]
            mats[m, hi:, hi:] = mats[m, hi:, hi:] - update[:, hi:]

    def basis_first():
        low_t[...] = jnp.zeros_like(low_t)
        mats[0, :256, :256] = take_lower(0)
        for m in range(2):
            mats[m, 256:, :256] = jnp.zeros((256, 256), jnp.float32)
        factor_blocks({0: 0})

    def basis_second():
        mats[0, :256, 256:] = take(1)
        mats[0, 256:, 256:] = take_lower(2)
        finish_block(0, 0)
        factor_blocks({0: 1})
        finish_block(0, 1)

    def corner_early():
        xcx, xcy = take_upper(0, 0), take_upper(2, 1)
        cap_mat[:256, :256] = xcx
        cap_mat[:256, 256:] = xcy
        cap_mat[256:, :256] = xcy
        part = sums[pl.ds(3 * WAVE, 256), :] * (1.0 / math.sqrt(drivers))
        forcing[:256, :] = part[:, :STEPS]
        forcing[256:, :] = part[:, STEPS:]

    def corner(g, ratio, gain):
        ratio = ratio * (1.0 / time_step)
        xcx, xcy = cap_mat[:256, :256], cap_mat[:256, 256:]
        cond_tail, ycy = take_lower(4), take_upper(4, 2)
        cap_mat[256:, 256:] = ycy
        mats[1, :256, :256] = g * xcy + ratio * xcx
        mats[1, :256, 256:] = g * ycy + ratio * xcy
        mats[1, 256:, 256:] = g * cond_tail + ratio * ycy

        def both(s, carry):
            factor_blocks({0: s + 2, 1: s})
            for i in range(2):

                @pl.when(s == i)
                def _():
                    finish_block(0, i + 2)
                    finish_block(1, i)

            return carry

        def alone(s, carry):
            factor_blocks({1: s})
            for i in range(2, 4):

                @pl.when(s == i)
                def _():
                    finish_block(1, i)

            return carry

        lax.fori_loop(0, 2, both, 0)
        lax.fori_loop(2, 4, alone, 0)
        next_map[...] = mats[0, 256:, :]
        low = split(mats[1], 2)
        half_way = sum_dot(low, split(cap_mat[...] * ratio, 2))
        power = sum_dot(split(half_way, 2), low, 1, 1)
        states = sum_dot(split(forcing[...] * gain, 2), low, 0, 1)
        time = lax.broadcasted_iota(jnp.int32, (STEPS, 512), 0)
        s = 1
        while s < STEPS:
            late = jnp.where(time >= s, pltpu.roll(states, s, 0), 0.0)
            parts = split(power, 2)
            late_parts = split(late, 2)
            if 2 * s < STEPS:
                both = sum_dot(
                    [jnp.concatenate([p, q], 0) for p, q in zip(parts, late_parts)], parts
                )
                power = both[:512]
                states = states + both[512:]
            else:
                states = states + sum_dot(late_parts, parts)
            s *= 2
        states = sum_dot(split(states, 2), low)
        response[...] = sum_dot(split(states, 2), split(low_t[...], 2), 1, 1)

    return basis_first, basis_second, corner_early, corner


def project_kernel(basis_in, krylov_in, next_map_in, second, basis, krylov, next_map, load_sem):
    loads = [
        pltpu.make_async_copy(src, dst, load_sem.at[i])
        for i, (src, dst) in enumerate(
            ((next_map_in, next_map), (basis_in, basis), (krylov_in, krylov))
        )
    ]
    for copy in loads:
        copy.start()
    loads[0].wait()
    maps = split(next_map[...], 2)
    loads[1].wait()
    loads[2].wait()
    for c in range(4):
        rows = pl.ds(c * 256, 256)
        second[rows, :] = sum_dot(
            split(basis[rows, :], 2), [m[:, :256] for m in maps], 1, 1
        ) + sum_dot(split(krylov[rows, :], 2), [m[:, 256:] for m in maps], 1, 1)


def project(basis, krylov, next_map):
    anywhere = pl.BlockSpec(memory_space=pltpu.HBM)
    f32 = jnp.float32
    return pl.pallas_call(
        project_kernel,
        out_shape=jax.ShapeDtypeStruct((NODES, K), f32),
        in_specs=[anywhere] * 3,
        out_specs=pl.BlockSpec(memory_space=pltpu.VMEM),
        scratch_shapes=[
            pltpu.VMEM((NODES, K), f32),
            pltpu.VMEM((NODES, K), f32),
            pltpu.VMEM((K, 2 * K), f32),
            pltpu.SemaphoreType.DMA((3,)),
        ],
        compiler_params=pltpu.CompilerParams(vmem_limit_bytes=65024 * 1024),
        cost_estimate=pl.CostEstimate(
            flops=2 * NODES * 2 * K * K * 3, bytes_accessed=4 * 2**20, transcendentals=0
        ),
        name="project",
    )(basis, krylov, next_map)


def shards(basis_start, admit, pattern, ground, capacity, ports, drive, corner_table, level_table):
    devices = lax.axis_size("gx") * lax.axis_size("gy")
    basis = basis_start.reshape(NODES, K)
    krylov, next_map, own = stats(
        NODES * devices, ports.shape[0] * devices,
        basis, admit, pattern, ground, capacity, ports, drive, corner_table, level_table,
    )
    swap = [(i, i ^ 1) for i in range(lax.axis_size("gx"))]
    other = lax.ppermute(own, "gx", swap)
    second = project(basis, krylov, next_map)
    even = lax.rem(lax.axis_index("gx"), 2) == 0
    response = jnp.stack([jnp.where(even, own, other), jnp.where(even, other, own)])
    return second.reshape(TX, TY, K), response


def solution(mesh):
    return jax.shard_map(
        shards,
        mesh=mesh,
        in_specs=(
            P("gx", "gy", None),
            P("gx", "gy"),
            P("gx", "gy"),
            P("gx", "gy"),
            P("gx", "gy"),
            P(("gx", "gy")),
            P(("gx", "gy"), None),
            P("gy", None),
            P(),
        ),
        out_specs=(P("gx", "gy", None), P("gy", None, None)),
        check_vma=False,
    )
```

```python
import functools
import math

import jax
import jax.numpy as jnp
from jax import lax
from jax.experimental import pallas as pl
from jax.experimental.pallas import tpu as pltpu
from jax.sharding import PartitionSpec as P

MESH = pl.DeviceIdType.MESH
highest = lax.Precision.HIGHEST
time_step = 0.25
K = 256
TX = 8
TY = 128
NODES = TX * TY
STEPS = 64
BLOCK = 128


def dot(a, b, ca=1, cb=0, precision=highest):
    return lax.dot_general(
        a, b, (((ca,), (cb,)), ((), ())), precision=precision, preferred_element_type=jnp.float32
    )


def place():
    gx, gy = lax.axis_index("gx"), lax.axis_index("gy")
    z = (gx // 4) * 2 + (gy % 4) // 2
    return gx, gy, gx % 4, gy // 4, z, gy % 2


def device(x, y, z, core):
    return ((z // 2) * 4 + x, y * 4 + (z % 2) * 2 + core)


WAVES = 5
WAVE = 512
HALF = 256
PIECE = 16


def stats_kernel(
    basis_in, admit_in, pattern_in, ground_in, capacity_in, ports_in, drive_in,
    corners_in, levels_in, y_copy, next_map, response, out,
    basis, admit, pattern, ground, capacity, ports, drive, corners, levels, load_sem,
    y_out, y_sem,
    strength, sx, left_send, right_send, tiles, halo_row, halo_col,
    top_send, edge_send, next_row, next_col,
    v, got_core, got_plane, got_z, send_sem, recv_sem, mats, low_t, cap_mat, forcing, work,
    *, nodes, drivers,
):
    gx, gy, x, y, z, core = place()
    up = (lax.rem(gx + 15, 16), gy)
    down = (lax.rem(gx + 1, 16), gy)
    left = (gx, lax.rem(gy + 15, 16))
    right = (gx, lax.rem(gy + 1, 16))
    sibling = device(x, y, z, 1 - core)
    plane = []
    for d in sorted(range(1, 16), key=lambda d: -min(d % 4, 4 - d % 4) - min(d // 4, 4 - d // 4)):
        px, py = lax.rem(x + d % 4, 4), lax.rem(y + d // 4, 4)
        plane.append((px * 4 + py, device(px, py, z, core)))
    along_z = [device(x, y, lax.rem(z + d, 8), core) for d in (4, 3, 5, 2, 6, 1, 7)]
    barrier = pltpu.get_barrier_semaphore()
    partners = [up, down, left, right, sibling] + [p[1] for p in plane] + along_z
    for partner in partners:
        pl.semaphore_signal(barrier, inc=1, device_id=partner, device_id_type=MESH)
    loads = [
        pltpu.make_async_copy(src, dst, load_sem.at[i])
        for i, (src, dst) in enumerate(
            (
                (basis_in, basis), (admit_in, admit), (pattern_in, pattern), (ground_in, ground),
                (capacity_in, capacity), (ports_in, ports), (drive_in, drive),
                (corners_in, corners), (levels_in, levels),
            )
        )
    ]
    for copy in loads:
        copy.start()

    started = []

    def send(src, dst, target):
        i = len(started)
        copy = pltpu.make_async_remote_copy(
            src_ref=src, dst_ref=dst, send_sem=send_sem.at[i], recv_sem=recv_sem.at[i],
            device_id=target, device_id_type=MESH,
        )
        copy.start()
        started.append(copy)
        return copy

    home = x * 4 + y
    flights = {}

    def span(ref, start, size):
        return ref.at[pl.ds(pl.multiple_of(start, 8), size), :]

    def start_core(w):
        start = w * WAVE + (1 - core) * HALF
        flights[w] = [send(span(v, start, HALF), got_core.at[w], sibling)]

    def landed(w):
        for copy in flights[w]:
            copy.wait_recv()

    def start_plane(w):
        landed(w)
        start = w * WAVE + core * HALF
        rows = pl.ds(pl.multiple_of(start, 8), HALF)
        v[rows, :] = v[rows, :] + got_core[w]
        flights[w] = [
            send(span(v, start + spot * PIECE, PIECE), got_plane.at[w, i], target)
            for i, (spot, target) in enumerate(plane)
        ]

    def start_z(w):
        landed(w)
        start = w * WAVE + core * HALF + home * PIECE
        total = v[pl.ds(pl.multiple_of(start, 8), PIECE), :]
        for i in range(15):
            total = total + got_plane[w, i]
        got_z[w, z] = total
        flights[w] = [send(got_z.at[w, z], got_z.at[w, z], target) for target in along_z]

    def start_back(w):
        landed(w)
        total = got_z[w, 0]
        for i in range(1, 8):
            total = total + got_z[w, i]
        start = w * WAVE + core * HALF + home * PIECE
        out[pl.ds(pl.multiple_of(start, 8), PIECE), :] = total
        flights[w] = [
            send(span(out, start, PIECE), span(out, start, PIECE), target) for _, target in plane
        ]

    def start_last(w):
        landed(w)
        start = w * WAVE + core * HALF
        flights[w] = [send(span(out, start, HALF), span(out, start, HALF), sibling)]

    def put(w, value):
        v[pl.ds(w * WAVE, 256), :] = value[:, :128]
        v[pl.ds(w * WAVE + 256, 256), :] = value[:, 128:]

    row_id = lax.broadcasted_iota(jnp.int32, (K, K), 0)
    col_id = lax.broadcasted_iota(jnp.int32, (K, K), 1)

    def put_pair(w, lower, upper):
        put(w, jnp.where(row_id >= col_id, lower, upper))

    def gram(left_parts, right_parts):
        return sum_dot(left_parts, right_parts, 1, 0, 4)

    for copy in loads:
        copy.wait()
    strength[...] = admit[...] * pattern[...].astype(jnp.float32)
    own = strength[...]
    own_t = own.T
    cap_t = capacity[...].T
    for r in range(TX):
        rows = pl.ds(r * TY, TY)
        weighted = own_t[:, r : r + 1] * basis[rows, :]
        sx[rows, :] = weighted
        left_send[r : r + 1, :] = weighted[0:1, :]
        right_send[r : r + 1, :] = weighted[TY - 1 : TY, :]

    def capped(ref):
        return jnp.concatenate(
            [cap_t[:, r : r + 1] * ref[pl.ds(r * TY, TY), :] for r in range(TX)], 0
        )

    x_parts = split(basis[...], 2)
    xt_parts = split(basis[...].T, 2)
    cap_x = capped(basis)
    put_pair(0, gram(xt_parts, x_parts), gram(xt_parts, split(cap_x, 2)))

    pl.semaphore_wait(barrier, len(partners))
    last = (TX - 1) * TY
    halo = [
        send(strength, tiles.at[0], down),
        send(strength, tiles.at[1], up),
        send(strength, tiles.at[2], right),
        send(strength, tiles.at[3], left),
        send(sx.at[pl.ds(last, TY), :], halo_row.at[0], down),
        send(sx.at[pl.ds(0, TY), :], halo_row.at[1], up),
        send(right_send, halo_col.at[0], right),
        send(left_send, halo_col.at[1], left),
    ]
    start_core(0)
    node = lax.broadcasted_iota(jnp.int32, (8, NODES), 1)
    driver = lax.broadcasted_iota(jnp.int32, (8, NODES), 0)
    spot = jnp.full((8, NODES), -1, jnp.int32)
    for d in range(8):
        spot = jnp.where(driver == d, ports[d], spot)
    picked = (node == spot).astype(jnp.float32)
    v[pl.ds(3 * WAVE, 256), 0:STEPS] = dot(dot(picked, basis[...]), drive[...], 0, 0)
    start_plane(0)

    for copy in halo:
        copy.wait_recv()
    has_up, has_down = gx > 0, gx < 15
    has_left, has_right = gy > 0, gy < 15
    above = jnp.where(has_up, tiles[0, TX - 1 : TX, :], 0.0)
    below = jnp.where(has_down, tiles[1, 0:1, :], 0.0)
    before = jnp.where(has_left, tiles[2, :, TY - 1 : TY], 0.0)
    after = jnp.where(has_right, tiles[3, :, 0:1], 0.0)
    degree = (
        jnp.concatenate([above, own[:-1]], 0)
        + jnp.concatenate([own[1:], below], 0)
        + jnp.concatenate([before, own[:, :-1]], 1)
        + jnp.concatenate([own[:, 1:], after], 1)
    )
    diagonal_t = (ground[...] + own * degree).T
    place_in_row = lax.broadcasted_iota(jnp.int32, (TY, K), 0)

    def moved_back(block, edge):
        return jnp.where(place_in_row == TY - 1, edge, pltpu.roll(block, TY - 1, 0))

    def moved_on(block, edge):
        return jnp.where(place_in_row == 0, edge, pltpu.roll(block, 1, 0))

    halo_up = jnp.where(has_up, halo_row[0], 0.0)
    halo_down = jnp.where(has_down, halo_row[1], 0.0)
    halo_left = jnp.where(has_left, halo_col[0], 0.0)
    halo_right = jnp.where(has_right, halo_col[1], 0.0)
    inverse_t = 1.0 / cap_t
    for r in range(TX):
        rows = pl.ds(r * TY, TY)
        here = sx[rows, :]
        total = moved_on(here, halo_left[r : r + 1]) + moved_back(here, halo_right[r : r + 1])
        total = total + (halo_up if r == 0 else sx[pl.ds((r - 1) * TY, TY), :])
        total = total + (halo_down if r == TX - 1 else sx[pl.ds((r + 1) * TY, TY), :])
        image = diagonal_t[:, r : r + 1] * basis[rows, :] - own_t[:, r : r + 1] * total
        krylov = image * inverse_t[:, r : r + 1]
        y_out[rows, :] = krylov
        weighted = own_t[:, r : r + 1] * krylov
        if r == 0:
            top_send[...] = weighted
        edge_send[r : r + 1, :] = weighted[0:1, :]
    y_store = pltpu.make_async_copy(y_out, y_copy, y_sem)
    y_store.start()
    border = [send(top_send, next_row, up), send(edge_send, next_col, left)]

    y_parts = split(y_out[...], 2)
    put(1, gram(xt_parts, y_parts))
    start_core(1)
    cap_y = capped(y_out)
    v[pl.ds(3 * WAVE, 256), STEPS:128] = dot(dot(picked, y_out[...]), drive[...], 0, 0)
    v[pl.ds(3 * WAVE + 256, 256), :] = jnp.zeros((256, 128), jnp.float32)
    for i, squares in enumerate(
        (basis[...] * cap_x, basis[...] * cap_y, y_out[...] * cap_y)
    ):
        along = jnp.sum(squares, axis=0, keepdims=True)
        v[3 * WAVE + 256 + 2 * i : 3 * WAVE + 257 + 2 * i, :] = along[:, :128]
        v[3 * WAVE + 257 + 2 * i : 3 * WAVE + 258 + 2 * i, :] = along[:, 128:]
    start_core(3)
    start_plane(1)
    yt_parts = split(y_out[...].T, 2)
    cap_parts = split(cap_y, 2)
    cross = gram(xt_parts, cap_parts)
    put_pair(2, gram(yt_parts, y_parts), 0.5 * (cross + cross.T))
    start_core(2)
    start_plane(3)
    start_z(0)
    tail = gram(yt_parts, cap_parts)
    start_plane(2)

    for copy in border:
        copy.wait_recv()
    for copy in halo:
        copy.wait_send()
    bottom = jnp.where(has_down, next_row[...], 0.0)
    side = jnp.where(has_right, next_col[...], 0.0)
    for r in range(TX):
        rows = pl.ds(r * TY, TY)
        sx[rows, :] = own_t[:, r : r + 1] * y_out[rows, :]
    for r in range(TX):
        rows = pl.ds(r * TY, TY)
        total = moved_back(sx[rows, :], side[r : r + 1])
        total = total + (bottom if r == TX - 1 else sx[pl.ds((r + 1) * TY, TY), :])
        sx[rows, :] = (
            0.5 * diagonal_t[:, r : r + 1] * y_out[rows, :] - own_t[:, r : r + 1] * total
        )
    start_z(1)
    half = gram(yt_parts, split(sx[...], 2))
    put_pair(4, half + half.T, tail)
    start_core(4)
    start_back(0)
    start_z(3)
    start_plane(4)
    start_z(2)
    start_back(1)
    start_last(0)
    start_back(3)
    start_back(2)
    start_z(4)
    basis_first, basis_second, corner_early, corner = solver(
        nodes, drivers, out, next_map, response, mats, low_t, cap_mat, forcing, work
    )
    landed(0)
    basis_first()
    for w in (1, 3, 2):
        start_last(w)
    start_back(4)
    for w in (1, 3, 2):
        landed(w)
    basis_second()
    start_last(4)
    corner_early()
    y_store.wait()
    for copy in started[len(halo) :]:
        copy.wait_send()
    landed(4)
    odd = lax.rem(gx, 2)
    scales = []
    for kind in range(3):
        pair = []
        for k in range(2):
            level = levels[kind, 0]
            for i in range(1, 4):
                level = jnp.where(corners[k, kind] == i, levels[kind, i], level)
            pair.append(level)
        scales.append(jnp.where(odd == 0, pair[0], pair[1]))
    corner(*scales)


def stats(nodes, drivers, basis, admit, pattern, ground, capacity, ports, drive, corners, levels):
    vmem = pl.BlockSpec(memory_space=pltpu.VMEM)
    anywhere = pl.BlockSpec(memory_space=pl.ANY)
    f32 = jnp.float32
    copies = 8 + 2 + WAVES * (1 + 15 + 7 + 15 + 1)
    return pl.pallas_call(
        functools.partial(stats_kernel, nodes=nodes, drivers=drivers),
        out_shape=(
            jax.ShapeDtypeStruct((NODES, K), f32),
            jax.ShapeDtypeStruct((K, 2 * K), f32),
            jax.ShapeDtypeStruct((STEPS, 2 * K), f32),
        ),
        in_specs=[anywhere] * 9,
        out_specs=(anywhere, vmem, vmem),
        scratch_shapes=[
            pltpu.VMEM((WAVES * WAVE, 128), f32),
            pltpu.VMEM((NODES, K), f32),
            pltpu.VMEM((TX, TY), f32),
            pltpu.VMEM((TX, TY), jnp.int32),
            pltpu.VMEM((TX, TY), f32),
            pltpu.VMEM((TX, TY), f32),
            pltpu.SMEM((8,), jnp.int32),
            pltpu.VMEM((8, STEPS), f32),
            pltpu.SMEM((2, 3), jnp.int32),
            pltpu.SMEM((3, 4), f32),
            pltpu.SemaphoreType.DMA((9,)),
            pltpu.VMEM((NODES, K), f32),
            pltpu.SemaphoreType.DMA,
            pltpu.VMEM((TX, TY), f32),
            pltpu.VMEM((NODES, K), f32),
            pltpu.VMEM((TX, K), f32),
            pltpu.VMEM((TX, K), f32),
            pltpu.VMEM((4, TX, TY), f32),
            pltpu.VMEM((2, TY, K), f32),
            pltpu.VMEM((2, TX, K), f32),
            pltpu.VMEM((TY, K), f32),
            pltpu.VMEM((TX, K), f32),
            pltpu.VMEM((TY, K), f32),
            pltpu.VMEM((TX, K), f32),
            pltpu.VMEM((WAVES * WAVE, 128), f32),
            pltpu.VMEM((WAVES, HALF, 128), f32),
            pltpu.VMEM((WAVES, 15, PIECE, 128), f32),
            pltpu.VMEM((WAVES, 8, PIECE, 128), f32),
            pltpu.SemaphoreType.DMA((copies,)),
            pltpu.SemaphoreType.DMA((copies,)),
            pltpu.VMEM((2, 512, 512), f32),
            pltpu.VMEM((512, 512), f32),
            pltpu.VMEM((512, 512), f32),
            pltpu.VMEM((512, STEPS), f32),
            pltpu.VMEM((2, BLOCK, 2 * BLOCK), f32),
        ],
        compiler_params=pltpu.CompilerParams(
            collective_id=0, has_side_effects=True, vmem_limit_bytes=65024 * 1024
        ),
        name="stats",
    )(basis, admit, pattern, ground, capacity, ports, drive, corners, levels)


def split(a, count):
    parts = []
    for _ in range(count - 1):
        part = a.astype(jnp.bfloat16)
        parts.append(part)
        a = a - part.astype(jnp.float32)
    return parts + [a.astype(jnp.bfloat16)]


PAIRS = {
    2: ((0, 0), (0, 1), (1, 0)),
    4: ((0, 0), (0, 1), (1, 0), (1, 1)),
    3: ((0, 0), (0, 1), (1, 0), (1, 1), (0, 2), (2, 0)),
}


def deep_dot(a, b, ca, cb, count=3):
    pairs = PAIRS[count]
    left = jnp.concatenate([a[i] for i, j in pairs], ca)
    right = jnp.concatenate([b[j] for i, j in pairs], cb)
    return lax.dot_general(
        left, right, (((ca,), (cb,)), ((), ())), preferred_element_type=jnp.float32
    )


def sum_dot(a, b, ca=1, cb=0, count=2):
    total = None
    for i, j in PAIRS[count]:
        term = lax.dot_general(
            a[i], b[j], (((ca,), (cb,)), ((), ())), preferred_element_type=jnp.float32
        )
        total = term if total is None else total + term
    return total


def solver(nodes, drivers, sums, next_map, response, mats, low_t, cap_mat, forcing, work):
    scale = 1.0 / nodes

    wide_row = lax.broadcasted_iota(jnp.int32, (K, K), 0)
    wide_col = lax.broadcasted_iota(jnp.int32, (K, K), 1)

    def take(w):
        start = w * WAVE
        return (
            jnp.concatenate([sums[pl.ds(start, 256), :], sums[pl.ds(start + 256, 256), :]], 1)
            * scale
        )

    def take_lower(w):
        both = take(w)
        return jnp.where(wide_row >= wide_col, both, both.T)

    def take_upper(w, place):
        both = take(w)
        at = 3 * WAVE + 256 + 2 * place
        diag = jnp.concatenate([sums[at : at + 1, :], sums[at + 1 : at + 2, :]], 1) * scale
        return jnp.where(
            wide_row < wide_col, both, jnp.where(wide_row == wide_col, diag, both.T)
        )

    sub = lax.broadcasted_iota(jnp.int32, (8, 128), 0)
    row_id = lax.broadcasted_iota(jnp.int32, (BLOCK, BLOCK), 0)
    col_id = lax.broadcasted_iota(jnp.int32, (BLOCK, BLOCK), 1)

    def eliminate(rows, lo, first):
        tiles = range(first, 4)
        at = lo + 8 * first
        cols = {
            t: [jnp.broadcast_to(rows[t][0][:, at + k : at + k + 1], (8, 128)) for k in range(8)]
            for t in tiles
        }
        pivots = None

        def spread(k, row):
            return jnp.broadcast_to(cols[first][k][row : row + 1, :], (8, 128))

        pivot = spread(0, 0)
        for i in range(8):
            inverse = 1.0 / pivot
            pivots = pivot if pivots is None else jnp.where(sub == i, pivot, pivots)
            if i < 7:
                ahead = spread(i + 1, i + 1) - (spread(i, i + 1) * spread(i + 1, i)) * inverse
            below = {t: cols[t][i] * inverse for t in tiles if t != first}
            below[first] = jnp.where(sub > i, cols[first][i], 0.0) * inverse
            for k in range(i + 1, 8):
                top = jnp.broadcast_to(cols[first][k][i : i + 1, :], (8, 128))
                for t in tiles:
                    cols[t][k] = cols[t][k] - below[t] * top
            for h in range(2):
                top = jnp.broadcast_to(rows[first][h][i : i + 1, :], (8, 128))
                for t in tiles:
                    rows[t][h] = rows[t][h] - below[t] * top
            pivot = ahead
        root = lax.rsqrt(pivots)
        return [rows[first][h] * root for h in range(2)]

    def factor_panel(lo, ms):
        done = lo + 32
        rows = {
            m: [[work[m, lo + 8 * t : lo + 8 * t + 8, h * 128 : h * 128 + 128] for h in range(2)]
                for t in range(4)]
            for m in ms
        }
        final = {m: [None] * 4 for m in ms}
        for t in range(4):
            for m in ms:
                final[m][t] = eliminate(rows[m], lo, t)
        for m in ms:
            panel = jnp.concatenate([jnp.concatenate(final[m][t], 1) for t in range(4)], 0)
            work[m, lo:done, :] = panel
            if done < BLOCK:
                parts = split(panel, 3)
                update = deep_dot([p[:, :BLOCK] for p in parts], parts, 0, 0)
                work[m, done:, :] = work[m, done:, :] - update[done:, :]

    def factor_blocks(places):
        for m, place in places.items():
            lo = pl.multiple_of(place * BLOCK, BLOCK)
            work[m, :, :BLOCK] = mats[m, pl.ds(lo, BLOCK), pl.ds(lo, BLOCK)]
            work[m, :, BLOCK:] = (row_id == col_id).astype(jnp.float32)
        for p in range(BLOCK // 32):
            factor_panel(32 * p, list(places))
        if 0 in places:
            lo = pl.multiple_of(places[0] * BLOCK, BLOCK)
            low_t[pl.ds(lo, BLOCK), pl.ds(lo, BLOCK)] = jnp.where(
                row_id <= col_id, work[0, :, :BLOCK], 0.0
            )

    def finish_block(m, i):
        lo, hi = i * BLOCK, (i + 1) * BLOCK
        corner = jnp.where(row_id >= col_id, work[m, :, BLOCK:], 0.0)
        row = deep_dot(split(corner, 3), split(mats[m, lo:hi, :], 3), 1, 0)
        if i > 0:
            mats[m, lo:hi, :lo] = row[:, :lo]
        mats[m, lo:hi, lo:hi] = corner
        if i < 3:
            mats[m, lo:hi, hi:] = jnp.zeros((BLOCK, 512 - hi), jnp.float32)
            if m == 0:
                low_t[lo:hi, hi:] = row[:, hi:]
            left = [row[:, :lo]] if i > 0 else []
            row = jnp.concatenate(left + [corner, row[:, hi:]], 1)
            parts = split(row, 3)
            update = deep_dot([p[:, hi:] for p in parts], parts, 0, 0)
            if i > 0:
                mats[m, hi:, :lo] = mats[m, hi:, :lo] - update[:, :lo]
            mats[m, hi:, lo:hi] = -update[:, lo:hi]
            mats[m, hi:, hi:] = mats[m, hi:, hi:] - update[:, hi:]

    def basis_first():
        low_t[...] = jnp.zeros_like(low_t)
        mats[0, :256, :256] = take_lower(0)
        for m in range(2):
            mats[m, 256:, :256] = jnp.zeros((256, 256), jnp.float32)
        factor_blocks({0: 0})

    def basis_second():
        mats[0, :256, 256:] = take(1)
        mats[0, 256:, 256:] = take_lower(2)
        finish_block(0, 0)
        factor_blocks({0: 1})
        finish_block(0, 1)

    def corner_early():
        xcx, xcy = take_upper(0, 0), take_upper(2, 1)
        cap_mat[:256, :256] = xcx
        cap_mat[:256, 256:] = xcy
        cap_mat[256:, :256] = xcy
        part = sums[pl.ds(3 * WAVE, 256), :] * (1.0 / math.sqrt(drivers))
        forcing[:256, :] = part[:, :STEPS]
        forcing[256:, :] = part[:, STEPS:]

    def corner(g, ratio, gain):
        ratio = ratio * (1.0 / time_step)
        xcx, xcy = cap_mat[:256, :256], cap_mat[:256, 256:]
        cond_tail, ycy = take_lower(4), take_upper(4, 2)
        cap_mat[256:, 256:] = ycy
        mats[1, :256, :256] = g * xcy + ratio * xcx
        mats[1, :256, 256:] = g * ycy + ratio * xcy
        mats[1, 256:, 256:] = g * cond_tail + ratio * ycy

        def both(s, carry):
            factor_blocks({0: s + 2, 1: s})
            for i in range(2):

                @pl.when(s == i)
                def _():
                    finish_block(0, i + 2)
                    finish_block(1, i)

            return carry

        def alone(s, carry):
            factor_blocks({1: s})
            for i in range(2, 4):

                @pl.when(s == i)
                def _():
                    finish_block(1, i)

            return carry

        lax.fori_loop(0, 2, both, 0)
        lax.fori_loop(2, 4, alone, 0)
        next_map[...] = mats[0, 256:, :]
        low = split(mats[1], 2)
        half_way = sum_dot(low, split(cap_mat[...] * ratio, 2))
        power = sum_dot(split(half_way, 2), low, 1, 1)
        states = sum_dot(split(forcing[...] * gain, 2), low, 0, 1)
        time = lax.broadcasted_iota(jnp.int32, (STEPS, 512), 0)
        s = 1
        while s < 16:
            late = jnp.where(time >= s, pltpu.roll(states, s, 0), 0.0)
            parts = split(power, 2)
            both = sum_dot(
                [jnp.concatenate([p, q], 0) for p, q in zip(parts, split(late, 2))], parts
            )
            power = both[:512]
            states = states + both[512:]
            s *= 2
        parts = split(power, 2)
        runs = [states[:s]]
        for first in range(s, STEPS, s):
            runs.append(states[first : first + s] + sum_dot(split(runs[-1], 2), parts))
        states = jnp.concatenate(runs, 0)
        states = sum_dot(split(states, 2), low)
        response[...] = sum_dot(split(states, 2), split(low_t[...], 2), 1, 1)

    return basis_first, basis_second, corner_early, corner


def project_kernel(basis_in, krylov_in, next_map_in, second, basis, krylov, next_map, load_sem):
    loads = [
        pltpu.make_async_copy(src, dst, load_sem.at[i])
        for i, (src, dst) in enumerate(
            ((next_map_in, next_map), (basis_in, basis), (krylov_in, krylov))
        )
    ]
    for copy in loads:
        copy.start()
    loads[0].wait()
    maps = split(next_map[...], 2)
    loads[1].wait()
    loads[2].wait()
    for c in range(4):
        rows = pl.ds(c * 256, 256)
        second[rows, :] = sum_dot(
            split(basis[rows, :], 2), [m[:, :256] for m in maps], 1, 1
        ) + sum_dot(split(krylov[rows, :], 2), [m[:, 256:] for m in maps], 1, 1)


def project(basis, krylov, next_map):
    anywhere = pl.BlockSpec(memory_space=pltpu.HBM)
    f32 = jnp.float32
    return pl.pallas_call(
        project_kernel,
        out_shape=jax.ShapeDtypeStruct((NODES, K), f32),
        in_specs=[anywhere] * 3,
        out_specs=pl.BlockSpec(memory_space=pltpu.VMEM),
        scratch_shapes=[
            pltpu.VMEM((NODES, K), f32),
            pltpu.VMEM((NODES, K), f32),
            pltpu.VMEM((K, 2 * K), f32),
            pltpu.SemaphoreType.DMA((3,)),
        ],
        compiler_params=pltpu.CompilerParams(vmem_limit_bytes=65024 * 1024),
        cost_estimate=pl.CostEstimate(
            flops=2 * NODES * 2 * K * K * 3, bytes_accessed=4 * 2**20, transcendentals=0
        ),
        name="project",
    )(basis, krylov, next_map)


def shards(basis_start, admit, pattern, ground, capacity, ports, drive, corner_table, level_table):
    devices = lax.axis_size("gx") * lax.axis_size("gy")
    basis = basis_start.reshape(NODES, K)
    krylov, next_map, own = stats(
        NODES * devices, ports.shape[0] * devices,
        basis, admit, pattern, ground, capacity, ports, drive, corner_table, level_table,
    )
    swap = [(i, i ^ 1) for i in range(lax.axis_size("gx"))]
    other = lax.ppermute(own, "gx", swap)
    second = project(basis, krylov, next_map)
    even = lax.rem(lax.axis_index("gx"), 2) == 0
    response = jnp.stack([jnp.where(even, own, other), jnp.where(even, other, own)])
    return second.reshape(TX, TY, K), response


def solution(mesh):
    return jax.shard_map(
        shards,
        mesh=mesh,
        in_specs=(
            P("gx", "gy", None),
            P("gx", "gy"),
            P("gx", "gy"),
            P("gx", "gy"),
            P("gx", "gy"),
            P(("gx", "gy")),
            P(("gx", "gy"), None),
            P("gy", None),
            P(),
        ),
        out_specs=(P("gx", "gy", None), P("gy", None, None)),
        check_vma=False,
    )
```
